128 devices in a mesh: sec: 2 (over x_hi), seq: 32 (over z, y, core), dp: 2 (over x_lo).
Axes of the slice: x: 4 (x_hi: 2, x_lo: 2; x = x_hi * 2 + x_lo), y: 4, z: 4, core: 2. Of those that a mesh axis runs over, the one named last changes fastest.
Arguments:
- q_heads: bfloat16 [2, 32768, 1024], P('dp', ('sec', 'seq')), may hold values from -6 to 6
- out_grad: bfloat16 [2, 32768, 1024], P('dp', ('sec', 'seq')), may hold values from -6 to 6
- memory: bfloat16 [2, 1024, 2048], P('dp', ('sec', 'seq')), may hold values from -6 to 6
- key_weight: bfloat16 [2048, 1024], replicated, may hold values from -0.125 to 0.125
- value_weight: bfloat16 [2048, 1024], replicated, may hold values from -0.125 to 0.125
- target_modality: int32 [2, 256], P('dp', ('sec', 'seq')), may hold values from 0 to 20
- memory_modality: int32 [2, 8], P('dp'), may hold values from 0 to 20
- allow_pairs: int32 [21, 21], replicated, may hold values 0 or 1
Outputs:
- q_grad: bfloat16 [2, 32768, 1024], P('dp', ('sec', 'seq'))
- memory_grad: bfloat16 [2, 1024, 2048], P('dp', ('sec', 'seq'))
- key_weight_grad: float32 [2048, 1024], P(('sec', 'seq', 'dp'))
- value_weight_grad: float32 [2048, 1024], P(('sec', 'seq', 'dp'))
The draws below stay inside these ranges and needn't reach their ends.
All inputs are finite; a program needn't handle non-finite values.
Results may differ from the reference program's by a relative error of at most 0.01.
Values may be sent and summed in bfloat16 or wider, within the bound.
No kernel may reach another device: no remote copies, remote signals or barrier semaphores. Data moves between devices by JAX's collectives and lax.ppermute only.
A program may use at most 128 MiB of HBM per device.

```python
import math
import jax
import jax.numpy as jnp
from jax import lax

D = 2048
HEADS = 16
HD = 64
BLOCK = 128
MODALITIES = 21
A = 1024
NQ = 32768
NM = 1024
SAMPLES = 2
N_DP = 2


def place_ends(result, rng, least, top_value):
    index_at = [jax.random.randint(jax.random.fold_in(rng, axis), (), 0, length) for axis, length in enumerate(result.shape)]
    widest = result.shape.index(max(result.shape))
    neighbour = index_at[:widest] + [(index_at[widest] + 1) % result.shape[widest]] + index_at[widest + 1:]
    return result.at[tuple(index_at)].set(least).at[tuple(neighbour)].set(top_value)


def block_scale(stream_key, extent, shards, low, top_value):
    def one(dim, shards_of):
        steps = jax.random.uniform(jax.random.fold_in(jax.random.fold_in(stream_key, 6), dim), (shards_of,), jnp.float32, low / len(shards), top_value / len(shards))
        return jnp.repeat(jnp.exp(steps), extent[dim] // shards_of).reshape((-1,) + (1,) * (len(extent) - dim - 1))

    gain = one(*shards[0])
    for cut in shards[1:]:
        gain = gain * one(*cut)
    return gain


def noise(stream_key, dims, deviation, limit, split=(), held_as=jnp.bfloat16):
    level = block_scale(stream_key, dims, split, -0.22, 0.18) if split else 1.0
    array = jax.random.normal(stream_key, dims, jnp.float32) * deviation * level
    return jnp.minimum(jnp.maximum(array, -limit), limit).astype(held_as)


def setup_inputs(seed: int = 0) -> dict:
    seeds = jax.random.split(jax.random.key(seed), 9)
    q_heads = noise(seeds[0], (SAMPLES, NQ, A), 1.0, 6.0, ((0, 2), (1, 64)))
    out_grad = noise(seeds[1], (SAMPLES, NQ, A), 1.0, 6.0, ((0, 2), (1, 64)))
    memory = noise(seeds[2], (SAMPLES, NM, D), 1.0, 6.0, ((0, 2), (1, 64)))
    key_weight = noise(seeds[3], (D, A), D ** -0.5, 0.125)
    value_weight = noise(seeds[4], (D, A), D ** -0.5, 0.125)
    target_modality = place_ends(jax.random.randint(seeds[5], (SAMPLES, NQ // BLOCK), 0, MODALITIES), jax.random.fold_in(seeds[5], 1), 0, MODALITIES - 1).astype(jnp.int32)
    memory_modality = place_ends(jax.random.randint(seeds[6], (SAMPLES, NM // BLOCK), 0, MODALITIES), jax.random.fold_in(seeds[6], 1), 0, MODALITIES - 1).astype(jnp.int32)
    allow_pairs = place_ends((jax.random.randint(seeds[7], (MODALITIES, MODALITIES), 0, 2) < 1).astype(jnp.int32), jax.random.fold_in(seeds[7], 1), 0, 1)
    return {"q_heads": q_heads, "out_grad": out_grad, "memory": memory, "key_weight": key_weight, "value_weight": value_weight, "target_modality": target_modality, "memory_modality": memory_modality, "allow_pairs": allow_pairs}


def head_grads(query, grad, keys, values, allowed, scale):
    scores = jnp.dot(query, keys.T, preferred_element_type=jnp.float32) * scale
    scores = jnp.where(allowed, scores, -1e+30)
    top = lax.optimization_barrier(jnp.max(scores, axis=1, keepdims=True))
    expd = jnp.where(allowed, jnp.exp(scores - top), 0.0)
    probs = expd / lax.optimization_barrier(jnp.sum(expd, axis=1, keepdims=True))
    probs_b = probs.astype(jnp.bfloat16)
    attended = jnp.dot(probs_b, values, preferred_element_type=jnp.float32)
    delta = lax.optimization_barrier(jnp.sum(grad.astype(jnp.float32) * attended, axis=1, keepdims=True))
    dprob = jnp.dot(grad, values.T, preferred_element_type=jnp.float32)
    score_grad = (probs * (dprob - delta)).astype(jnp.bfloat16)
    qgrad = jnp.dot(score_grad, keys, preferred_element_type=jnp.float32) * scale
    kgrad = jnp.dot(score_grad.T, query, preferred_element_type=jnp.float32) * scale
    vgrad = jnp.dot(probs_b.T, grad, preferred_element_type=jnp.float32)
    return (qgrad, kgrad, vgrad)

def reference(q_heads, out_grad, memory, key_weight, value_weight, target_modality, memory_modality, allow_pairs):
    scale = 1.0 / math.sqrt(HD)
    q_list = []
    m_list = []
    wk_total = jnp.zeros((D, HEADS * HD), jnp.float32)
    wv_total = jnp.zeros((D, HEADS * HD), jnp.float32)
    for sample in range(N_DP):
        keys = jnp.dot(memory[sample], key_weight, preferred_element_type=jnp.float32).astype(jnp.bfloat16)
        values = jnp.dot(memory[sample], value_weight, preferred_element_type=jnp.float32).astype(jnp.bfloat16)
        q_mods = jnp.repeat(target_modality[sample], BLOCK)
        k_mods = jnp.repeat(memory_modality[sample], BLOCK)
        first = jnp.arange(keys.shape[0], dtype=jnp.int32) < BLOCK
        allowed = (allow_pairs[q_mods[:, None], k_mods[None, :]] == 1) | first[None, :]
        queries = q_heads[sample]
        grads = out_grad[sample]

        def one_head(head):
            start = (head * HD).astype(jnp.int32)
            query = lax.dynamic_slice_in_dim(queries, start, HD, 1)
            grad = lax.dynamic_slice_in_dim(grads, start, HD, 1)
            kslice = lax.dynamic_slice_in_dim(keys, start, HD, 1)
            vslice = lax.dynamic_slice_in_dim(values, start, HD, 1)
            return head_grads(query, grad, kslice, vslice, allowed, scale)
        qgrad, kgrad, vgrad = lax.map(one_head, jnp.arange(HEADS, dtype=jnp.int32))
        qgrad = jnp.transpose(qgrad, (1, 0, 2)).reshape(queries.shape[0], HEADS * HD)
        kgrad = jnp.transpose(kgrad, (1, 0, 2)).reshape(keys.shape[0], HEADS * HD).astype(jnp.bfloat16)
        vgrad = jnp.transpose(vgrad, (1, 0, 2)).reshape(keys.shape[0], HEADS * HD).astype(jnp.bfloat16)
        q_list.append(qgrad.astype(jnp.bfloat16))
        mgrad = jnp.dot(kgrad, key_weight.T, preferred_element_type=jnp.float32) + jnp.dot(vgrad, value_weight.T, preferred_element_type=jnp.float32)
        m_list.append(mgrad.astype(jnp.bfloat16))
        wk_total = wk_total + jnp.dot(memory[sample].T, kgrad, preferred_element_type=jnp.float32)
        wv_total = wv_total + jnp.dot(memory[sample].T, vgrad, preferred_element_type=jnp.float32)
    return (jnp.stack(q_list), jnp.stack(m_list), wk_total, wv_total)
```

```python
import functools

import jax
import jax.numpy as jnp
from jax import lax
from jax.experimental import pallas as pl
from jax.experimental.pallas import tpu as pltpu
from jax.sharding import Mesh, PartitionSpec as P

HD = 64
BLOCK = 128
LANES = 128
SCALE = 0.125
CHUNK = 256
NT = (((1,), (1,)), ((), ()))
NN = (((1,), (0,)), ((), ()))
TN = (((0,), (0,)), ((), ()))
HEAD_AXES = ("sec", "y", "core")
SAMPLE_AXES = ("sec", "z", "y", "core")
ALL_AXES = ("sec", "z", "y", "core", "dp")
bf16 = jnp.bfloat16
f32 = jnp.float32


def dot(a, b, dims):
    return lax.dot_general(a, b, dims, preferred_element_type=f32)


def low_half():
    return lax.broadcasted_iota(jnp.int32, (1, LANES), 1) < HD


def swap_halves(a, b):
    lo = low_half()
    return jnp.where(lo, a, pltpu.roll(b, HD, 1)), jnp.where(lo, pltpu.roll(a, HD, 1), b)


def params(**kw):
    return pltpu.CompilerParams(vmem_limit_bytes=48 << 20, **kw)


def pack_kernel(q_ref, g_ref, mask_ref, out_ref):
    for k, ref in enumerate((q_ref, g_ref)):
        for t in range(2):
            a = ref[0, t * 256 : t * 256 + 128, :].astype(f32)
            b = ref[0, t * 256 + 128 : t * 256 + 256, :].astype(f32)
            even, odd = swap_halves(a, b)
            rows = slice(k * 256 + t * 128, k * 256 + t * 128 + 128)
            out_ref[0, rows, :] = even.astype(bf16)
            out_ref[1, rows, :] = odd.astype(bf16)
    out_ref[0, 512:528, :] = mask_ref[...]
    out_ref[1, 512:528, :] = mask_ref[...]


def pack_targets(q, g, mask):
    pairs = q.shape[2] // LANES
    return pl.pallas_call(
        pack_kernel,
        grid=(pairs,),
        in_specs=[
            pl.BlockSpec((1, 512, LANES), lambda p: (0, 0, p)),
            pl.BlockSpec((1, 512, LANES), lambda p: (0, 0, p)),
            pl.BlockSpec((16, LANES), lambda p: (0, 0)),
        ],
        out_specs=pl.BlockSpec((2, 528, LANES), lambda p: (p, 0, 0)),
        out_shape=jax.ShapeDtypeStruct((2 * pairs, 528, LANES), bf16),
        compiler_params=params(),
        cost_estimate=pl.CostEstimate(flops=0, bytes_accessed=5 << 20, transcendentals=0),
        name="pack_targets",
    )(q, g, mask)


def unpack_kernel(in_ref, out_ref):
    for t in range(2):
        even = in_ref[0, t * 128 : t * 128 + 128, :].astype(f32)
        odd = in_ref[1, t * 128 : t * 128 + 128, :].astype(f32)
        a, b = swap_halves(even, odd)
        out_ref[0, t * 256 : t * 256 + 128, :] = a.astype(bf16)
        out_ref[0, t * 256 + 128 : t * 256 + 256, :] = b.astype(bf16)


def unpack_targets(x):
    pairs = x.shape[0] // 2
    return pl.pallas_call(
        unpack_kernel,
        grid=(pairs,),
        in_specs=[pl.BlockSpec((2, 256, LANES), lambda p: (p, 0, 0))],
        out_specs=pl.BlockSpec((1, 512, LANES), lambda p: (0, 0, p)),
        out_shape=jax.ShapeDtypeStruct((1, 512, pairs * LANES), bf16),
        compiler_params=params(),
        cost_estimate=pl.CostEstimate(flops=0, bytes_accessed=2 << 20, transcendentals=0),
        name="unpack_targets",
    )(x)


def project_kernel(mem_ref, wk_ref, wv_ref, out_ref):
    mem = mem_ref[0]
    k = dot(mem, wk_ref[...], NN)
    v = dot(mem, wv_ref[...], NN)
    even, odd = swap_halves(k, v)
    for z in range(4):
        out_ref[0, z, 0] = even.astype(bf16)
        out_ref[0, z, 1] = odd.astype(bf16)


def project(mem, wk, wv):
    d = wk.shape[0]
    return pl.pallas_call(
        project_kernel,
        grid=(8,),
        in_specs=[
            pl.BlockSpec((1, 16, d), lambda p: (0, 0, 0)),
            pl.BlockSpec((d, LANES), lambda p: (0, p)),
            pl.BlockSpec((d, LANES), lambda p: (0, p)),
        ],
        out_specs=pl.BlockSpec((1, 4, 2, 16, LANES), lambda p: (p // 4, 0, p % 4, 0, 0)),
        out_shape=jax.ShapeDtypeStruct((2, 4, 8, 16, LANES), bf16),
        compiler_params=params(),
        cost_estimate=pl.CostEstimate(flops=0, bytes_accessed=9 << 20, transcendentals=0),
        name="project",
    )(mem, wk, wv)


def attend_kernel(mask_ref, kv_ref, r_ref, qg_ref, kvg_ref, k2_ref, v2_ref, kt_ref, ka_ref, va_ref):
    step = pl.program_id(0)
    last = pl.num_programs(0) - 1
    lo = low_half()
    left = lax.broadcasted_iota(jnp.int32, (1, 2 * LANES), 1) < LANES
    n = kv_ref.shape[0]
    per = CHUNK // BLOCK
    chunks = n // CHUNK

    @pl.when(step == 0)
    def _():
        kv = kv_ref[...].astype(f32)
        swapped = pltpu.roll(kv, HD, 1)
        k2 = jnp.where(lo, kv, swapped)
        k2_ref[...] = k2.astype(bf16)
        v2_ref[...] = jnp.where(lo, swapped, kv).astype(bf16)
        kt_ref[...] = jnp.transpose(k2)[:HD].astype(bf16)
        ka_ref[...] = jnp.zeros_like(ka_ref)
        va_ref[...] = jnp.zeros_like(va_ref)

    for t in range(2):
        q = r_ref[0, t * 128 : t * 128 + 128, :] * jnp.asarray(SCALE, bf16)
        g = r_ref[0, 256 + t * 128 : 256 + t * 128 + 128, :]
        zero = jnp.zeros_like(q)
        q2 = jnp.concatenate([jnp.where(lo, q, zero), jnp.where(lo, zero, q)], 0)
        g2 = jnp.concatenate([jnp.where(lo, g, zero), jnp.where(lo, zero, g)], 0)
        rows = [slice(c * CHUNK, c * CHUNK + CHUNK) for c in range(chunks)]
        scores = [dot(k2_ref[r, :], q2, NT) for r in rows]
        block = step * 4 + 2 * t
        hidden = []
        top = None
        for j in range(n // BLOCK):
            part = scores[j // per][(j % per) * BLOCK : (j % per + 1) * BLOCK]
            hide = jnp.where(
                left,
                jnp.where(mask_ref[block, j] > 0, 0.0, 1e30),
                jnp.where(mask_ref[block + 1, j] > 0, 0.0, 1e30),
            )
            hidden.append(hide)
            part_top = jnp.max(part, axis=0, keepdims=True) - hide
            top = part_top if top is None else jnp.maximum(top, part_top)
        expd = []
        total = None
        for c in range(chunks):
            parts = [
                jnp.exp(scores[c][i * BLOCK : (i + 1) * BLOCK] - (top + hidden[c * per + i]))
                for i in range(per)
            ]
            e = jnp.concatenate(parts, 0)
            expd.append(e)
            s = jnp.sum(e, axis=0, keepdims=True)
            total = s if total is None else total + s
        inverse = 1.0 / total
        dprobs = []
        delta = None
        for c in range(chunks):
            dp = dot(v2_ref[rows[c], :], g2, NT)
            dprobs.append(dp)
            s = jnp.sum(expd[c] * dp, axis=0, keepdims=True)
            delta = s if delta is None else delta + s
        delta = delta * inverse
        qgt = None
        for c in range(chunks):
            p = expd[c] * inverse
            ds = (p * (dprobs[c] - delta)).astype(bf16)
            va_ref[rows[c], :] += dot(p.astype(bf16), g2, NN)
            ka_ref[rows[c], :] += dot(ds, q2, NN)
            x = dot(kt_ref[:, rows[c]], ds, NN)
            qgt = x if qgt is None else qgt + x
        qgt = qgt * SCALE
        both = jnp.concatenate([qgt[:, :LANES], qgt[:, LANES:]], 0)
        qg_ref[0, t * 128 : t * 128 + 128, :] = jnp.transpose(both).astype(bf16)

    @pl.when(step == last)
    def _():
        ka = ka_ref[...]
        va = va_ref[...]
        ka = ka + pltpu.roll(ka, HD, 1)
        va = va + pltpu.roll(va, HD, 1)
        kvg_ref[...] = jnp.where(lo, ka, va).astype(bf16)


def attend(mask, kv, r):
    n = kv.shape[0]
    sources = r.shape[0]
    return pl.pallas_call(
        attend_kernel,
        grid_spec=pltpu.PrefetchScalarGridSpec(
            num_scalar_prefetch=1,
            grid=(sources,),
            in_specs=[
                pl.BlockSpec((n, LANES), lambda i, m: (0, 0)),
                pl.BlockSpec((1,) + r.shape[1:], lambda i, m: (i, 0, 0)),
            ],
            out_specs=[
                pl.BlockSpec((1, 256, LANES), lambda i, m: (i, 0, 0)),
                pl.BlockSpec((n, LANES), lambda i, m: (0, 0)),
            ],
            scratch_shapes=[
                pltpu.VMEM((n, LANES), bf16),
                pltpu.VMEM((n, LANES), bf16),
                pltpu.VMEM((HD, n), bf16),
                pltpu.VMEM((n, LANES), f32),
                pltpu.VMEM((n, LANES), f32),
            ],
        ),
        out_shape=[
            jax.ShapeDtypeStruct((sources, 256, LANES), bf16),
            jax.ShapeDtypeStruct((n, LANES), bf16),
        ],
        compiler_params=params(dimension_semantics=("arbitrary",)),
        cost_estimate=pl.CostEstimate(
            flops=45_000_000_000, bytes_accessed=4 << 20, transcendentals=0
        ),
        name="attend",
    )(mask, kv, r)


def memory_kernel(g_ref, wk_ref, wv_ref, out_ref, acc_ref):
    p = pl.program_id(0)
    kg, vg = swap_halves(g_ref[0].astype(f32), g_ref[1].astype(f32))
    part = dot(kg.astype(bf16), wk_ref[...], NT) + dot(vg.astype(bf16), wv_ref[...], NT)

    @pl.when(p == 0)
    def _():
        acc_ref[...] = part

    @pl.when(p > 0)
    def _():
        acc_ref[...] += part

    @pl.when(p == pl.num_programs(0) - 1)
    def _():
        out_ref[0] = acc_ref[...].astype(bf16)


def memory_grad(g, wk, wv):
    d = wk.shape[0]
    return pl.pallas_call(
        memory_kernel,
        grid=(8,),
        in_specs=[
            pl.BlockSpec((2, 16, LANES), lambda p: (p, 0, 0)),
            pl.BlockSpec((d, LANES), lambda p: (0, p)),
            pl.BlockSpec((d, LANES), lambda p: (0, p)),
        ],
        out_specs=pl.BlockSpec((1, 16, d), lambda p: (0, 0, 0)),
        out_shape=jax.ShapeDtypeStruct((1, 16, d), bf16),
        scratch_shapes=[pltpu.VMEM((16, d), f32)],
        compiler_params=params(dimension_semantics=("arbitrary",)),
        cost_estimate=pl.CostEstimate(flops=0, bytes_accessed=9 << 20, transcendentals=0),
        name="memory_grad",
    )(g, wk, wv)


def weight_kernel(in_ref, wk_ref, wv_ref):
    for p in range(8):
        even = in_ref[4 * p] + in_ref[4 * p + 1]
        odd = in_ref[4 * p + 2] + in_ref[4 * p + 3]
        k, v = swap_halves(even, odd)
        wk_ref[:, p * LANES : (p + 1) * LANES] = k
        wv_ref[:, p * LANES : (p + 1) * LANES] = v


def weight_grads(x):
    shape = jax.ShapeDtypeStruct((16, 8 * LANES), f32)
    return pl.pallas_call(
        weight_kernel, out_shape=[shape, shape], compiler_params=params(), name="weight_grads"
    )(x)


def exchange(x, axes):
    return lax.all_to_all(x, axes, 0, 0, tiled=True)


def body(q, g, mem, wk, wv, target_modality, memory_modality, allow_pairs):
    kinds = allow_pairs.shape[0]
    labels = jnp.arange(kinds, dtype=jnp.int32)
    q_onehot = (target_modality[0][:, None] == labels[None, :]).astype(f32)
    k_onehot = (memory_modality[0][:, None] == labels[None, :]).astype(f32)
    block_rows = jnp.dot(q_onehot, allow_pairs.astype(f32))
    block_mask = jnp.dot(block_rows, k_onehot.T) > 0.5
    first_block = jnp.arange(block_mask.shape[1], dtype=jnp.int32) == 0
    block_mask = (block_mask | first_block[None, :]).astype(bf16)
    blocks = block_mask.shape[1]
    mask_rows = jnp.pad(block_mask, ((0, 16 - block_mask.shape[0]), (0, LANES - blocks)))

    kv_blocks = project(mem, wk, wv).reshape(64, 16, LANES)
    kv = exchange(kv_blocks, SAMPLE_AXES).reshape(1024, LANES)
    targets = exchange(pack_targets(q, g, mask_rows), HEAD_AXES)
    mask = targets[:, 512:516, :blocks].reshape(64, blocks).astype(jnp.int32)

    columns = mem[0].reshape(16, 2, 4, 256).transpose(2, 0, 1, 3).reshape(1, 4, 1, 16, 512)
    columns, targets = lax.optimization_barrier((columns, targets))
    columns = jnp.broadcast_to(columns, (2, 4, 8, 16, 512)).reshape(64, 16, 512)
    columns = exchange(columns, SAMPLE_AXES).reshape(1024, 512)

    q_grad, part = attend(mask, kv, targets)
    q_grad = unpack_targets(exchange(q_grad, HEAD_AXES))

    around = [lax.ppermute(part, "z", [(i, (i + k) % 4) for i in range(4)]) for k in (1, 3, 2)]
    total = part.astype(f32)
    for x in around:
        total = total + x.astype(f32)
    total = total.astype(bf16)

    here = lax.axis_index("z")
    tokens = total.reshape(2, 4, 8, 16, LANES)
    tokens = lax.dynamic_index_in_dim(tokens, here, 1, keepdims=False).reshape(16, 16, LANES)
    m_grad = memory_grad(exchange(tokens, HEAD_AXES), wk, wv)

    w_part = dot(columns, total, TN).reshape(32, 16, LANES)
    wk_grad, wv_grad = weight_grads(exchange(w_part, ("sec", "y", "core", "dp")))
    return q_grad, m_grad, wk_grad, wv_grad


def solution(mesh):
    fine = Mesh(mesh.devices.reshape(2, 4, 4, 2, 2), ALL_AXES)
    rows = P("dp", SAMPLE_AXES, None)
    in_specs = (rows, rows, rows, P(), P(), P("dp", SAMPLE_AXES), P("dp", None), P())
    out_specs = (rows, rows, P(ALL_AXES, None), P(ALL_AXES, None))
    return jax.shard_map(body, mesh=fine, in_specs=in_specs, out_specs=out_specs, check_vma=False)
```

```python
import functools

import jax
import jax.numpy as jnp
from jax import lax
from jax.experimental import pallas as pl
from jax.experimental.pallas import tpu as pltpu
from jax.sharding import Mesh, PartitionSpec as P

HD = 64
BLOCK = 128
LANES = 128
SCALE = 0.125
CHUNK = 256
NT = (((1,), (1,)), ((), ()))
NN = (((1,), (0,)), ((), ()))
TN = (((0,), (0,)), ((), ()))
HEAD_AXES = ("sec", "y", "core")
SAMPLE_AXES = ("sec", "z", "y", "core")
ALL_AXES = ("sec", "z", "y", "core", "dp")
bf16 = jnp.bfloat16
f32 = jnp.float32


def dot(a, b, dims):
    return lax.dot_general(a, b, dims, preferred_element_type=f32)


def low_half():
    return lax.broadcasted_iota(jnp.int32, (1, LANES), 1) < HD


def swap_halves(a, b):
    lo = low_half()
    return jnp.where(lo, a, pltpu.roll(b, HD, 1)), jnp.where(lo, pltpu.roll(a, HD, 1), b)


def params(mib=48, **kw):
    return pltpu.CompilerParams(vmem_limit_bytes=mib << 20, **kw)


ROWS = 608


def pack_kernel(q_ref, g_ref, hide_ref, out_ref):
    for i in range(2):
        cols = slice(i * LANES, (i + 1) * LANES)
        for k, ref in enumerate((q_ref, g_ref)):
            for t in range(2):
                a = ref[0, t * 256 : t * 256 + 128, cols].astype(f32)
                b = ref[0, t * 256 + 128 : t * 256 + 256, cols].astype(f32)
                even, odd = swap_halves(a, b)
                rows = slice(k * 256 + t * 128, k * 256 + t * 128 + 128)
                out_ref[2 * i, rows, :] = even.astype(bf16)
                out_ref[2 * i + 1, rows, :] = odd.astype(bf16)
    for i in range(4):
        out_ref[i, 512:576, :] = jnp.zeros((64, LANES), bf16)
        out_ref[i, 576:608, :] = hide_ref[...]


def pack_targets(q, g, hide):
    return pl.pallas_call(
        pack_kernel,
        grid=(4,),
        in_specs=[
            pl.BlockSpec((1, 512, 256), lambda p: (0, 0, p)),
            pl.BlockSpec((1, 512, 256), lambda p: (0, 0, p)),
            pl.BlockSpec((32, LANES), lambda p: (0, 0)),
        ],
        out_specs=pl.BlockSpec((4, ROWS, LANES), lambda p: (p, 0, 0)),
        out_shape=jax.ShapeDtypeStruct((16, ROWS, LANES), bf16),
        compiler_params=params(),
        cost_estimate=pl.CostEstimate(flops=0, bytes_accessed=9 << 20, transcendentals=0),
        name="pack_targets",
    )(q, g, hide)


def project_kernel(z_ref, m0_ref, m1_ref, m2_ref, m3_ref, wk_ref, wv_ref, _, out_ref):
    mem = jnp.concatenate([m0_ref[0], m1_ref[0], m2_ref[0], m3_ref[0]], 0)
    k = dot(mem, wk_ref[...], NN)
    v = dot(mem, wv_ref[...], NN)
    for i in range(2):
        cols = slice(i * LANES, (i + 1) * LANES)
        even, odd = swap_halves(k[:, cols], v[:, cols])
        for j in range(4):
            at = pl.multiple_of(lax.rem(z_ref[0] + 4 - j, 4) * 16, 16)
            out_ref[2 * i, pl.ds(at, 16), :] = even[j * 16 : j * 16 + 16].astype(bf16)
            out_ref[2 * i + 1, pl.ds(at, 16), :] = odd[j * 16 : j * 16 + 16].astype(bf16)


def project(z, mems, wk, wv, payload):
    d = wk.shape[0]
    mem_spec = pl.BlockSpec((1, 16, d), lambda p, z: (0, 0, 0))
    w_spec = pl.BlockSpec((d, 256), lambda p, z: (0, p))
    return pl.pallas_call(
        project_kernel,
        grid_spec=pltpu.PrefetchScalarGridSpec(
            num_scalar_prefetch=1,
            grid=(4,),
            in_specs=[mem_spec] * 4 + [w_spec] * 2 + [pl.BlockSpec(memory_space=pl.ANY)],
            out_specs=pl.BlockSpec((4, 64, LANES), lambda p, z: (p, 8, 0)),
        ),
        out_shape=jax.ShapeDtypeStruct(payload.shape, bf16),
        input_output_aliases={7: 0},
        compiler_params=params(),
        cost_estimate=pl.CostEstimate(flops=0, bytes_accessed=12 << 20, transcendentals=0),
        name="project",
    )(z, *mems, wk, wv, payload)


def unpack_kernel(in_ref, out_ref):
    for i in range(2):
        for t in range(2):
            even = in_ref[2 * i, t * 128 : t * 128 + 128, :].astype(f32)
            odd = in_ref[2 * i + 1, t * 128 : t * 128 + 128, :].astype(f32)
            a, b = swap_halves(even, odd)
            cols = slice(i * LANES, (i + 1) * LANES)
            out_ref[0, t * 256 : t * 256 + 128, cols] = a.astype(bf16)
            out_ref[0, t * 256 + 128 : t * 256 + 256, cols] = b.astype(bf16)


def unpack_targets(x):
    return pl.pallas_call(
        unpack_kernel,
        grid=(4,),
        in_specs=[pl.BlockSpec((4, 256, LANES), lambda p: (p, 0, 0))],
        out_specs=pl.BlockSpec((1, 512, 256), lambda p: (0, 0, p)),
        out_shape=jax.ShapeDtypeStruct((1, 512, 1024), bf16),
        compiler_params=params(),
        cost_estimate=pl.CostEstimate(flops=0, bytes_accessed=6 << 20, transcendentals=0),
        name="unpack_targets",
    )(x)


def attend_kernel(kv_ref, r_ref, qg_ref, kvg_ref, k2_ref, v2_ref, kt_ref, ka_ref, va_ref):
    step = pl.program_id(0)
    last = pl.num_programs(0) - 1
    lo = low_half()
    n = k2_ref.shape[0]
    per = CHUNK // BLOCK
    chunks = n // CHUNK

    @pl.when(step == 0)
    def _():
        order = [(c, z) for c in (0, 8) for z in range(4)]
        kv = jnp.concatenate(
            [kv_ref[c + i, z * 16 : z * 16 + 16, :] for c, z in order for i in range(8)], 0
        ).astype(f32)
        swapped = pltpu.roll(kv, HD, 1)
        k2 = jnp.where(lo, kv, swapped)
        k2_ref[...] = k2.astype(bf16)
        v2_ref[...] = jnp.where(lo, swapped, kv).astype(bf16)
        kt_ref[...] = jnp.transpose(k2)[:HD].astype(bf16)
        ka_ref[...] = jnp.zeros_like(ka_ref)
        va_ref[...] = jnp.zeros_like(va_ref)

    for t in range(2):
        q = r_ref[0, t * 128 : t * 128 + 128, :] * jnp.asarray(SCALE, bf16)
        g = r_ref[0, 256 + t * 128 : 256 + t * 128 + 128, :]
        zero = jnp.zeros_like(q)
        q2 = jnp.concatenate([jnp.where(lo, q, zero), jnp.where(lo, zero, q)], 0)
        g2 = jnp.concatenate([jnp.where(lo, g, zero), jnp.where(lo, zero, g)], 0)
        rows = [slice(c * CHUNK, c * CHUNK + CHUNK) for c in range(chunks)]
        scores = [dot(k2_ref[r, :], q2, NT) for r in rows]
        away = r_ref[0, 576 + t * 16 : 576 + t * 16 + 16, :].astype(f32)
        hidden = []
        top = None
        for j in range(n // BLOCK):
            part = scores[j // per][(j % per) * BLOCK : (j % per + 1) * BLOCK]
            hide = jnp.concatenate([away[j : j + 1], away[8 + j : 9 + j]], 1)
            hidden.append(hide)
            part_top = jnp.max(part, axis=0, keepdims=True) - hide
            top = part_top if top is None else jnp.maximum(top, part_top)
        expd = []
        total = None
        for c in range(chunks):
            parts = [
                jnp.exp(scores[c][i * BLOCK : (i + 1) * BLOCK] - (top + hidden[c * per + i]))
                for i in range(per)
            ]
            e = jnp.concatenate(parts, 0)
            expd.append(e)
            s = jnp.sum(e, axis=0, keepdims=True)
            total = s if total is None else total + s
        inverse = 1.0 / total
        dprobs = []
        delta = None
        for c in range(chunks):
            dp = dot(v2_ref[rows[c], :], g2, NT)
            dprobs.append(dp)
            s = jnp.sum(expd[c] * dp, axis=0, keepdims=True)
            delta = s if delta is None else delta + s
        delta = delta * inverse
        qgt = None
        for c in range(chunks):
            p = expd[c] * inverse
            ds = (p * (dprobs[c] - delta)).astype(bf16)
            va_ref[rows[c], :] += dot(p.astype(bf16), g2, NN)
            ka_ref[rows[c], :] += dot(ds, q2, NN)
            x = dot(kt_ref[:, rows[c]], ds, NN)
            qgt = x if qgt is None else qgt + x
        qgt = qgt * SCALE
        both = jnp.concatenate([qgt[:, :LANES], qgt[:, LANES:]], 0)
        qg_ref[0, t * 128 : t * 128 + 128, :] = jnp.transpose(both).astype(bf16)

    @pl.when(step == last)
    def _():
        ka = ka_ref[...]
        va = va_ref[...]
        ka = ka + pltpu.roll(ka, HD, 1)
        va = va + pltpu.roll(va, HD, 1)
        kvg_ref[...] = jnp.where(lo, ka, va).astype(bf16)


def attend(r):
    sources = r.shape[0]
    n = 64 * sources
    return pl.pallas_call(
        attend_kernel,
        grid=(sources,),
        in_specs=[
            pl.BlockSpec((sources, 64, LANES), lambda i: (0, 8, 0)),
            pl.BlockSpec((1, ROWS, LANES), lambda i: (i, 0, 0)),
        ],
        out_specs=[
            pl.BlockSpec((1, 256, LANES), lambda i: (i, 0, 0)),
            pl.BlockSpec((n, LANES), lambda i: (0, 0)),
        ],
        scratch_shapes=[
            pltpu.VMEM((n, LANES), bf16),
            pltpu.VMEM((n, LANES), bf16),
            pltpu.VMEM((HD, n), bf16),
            pltpu.VMEM((n, LANES), f32),
            pltpu.VMEM((n, LANES), f32),
        ],
        out_shape=[
            jax.ShapeDtypeStruct((sources, 256, LANES), bf16),
            jax.ShapeDtypeStruct((n, LANES), bf16),
        ],
        compiler_params=params(dimension_semantics=("arbitrary",)),
        cost_estimate=pl.CostEstimate(
            flops=45_000_000_000, bytes_accessed=4 << 20, transcendentals=0
        ),
        name="attend",
    )(r, r)


def weight_kernel(z_ref, p0_ref, p1_ref, p2_ref, p3_ref, mem_ref, out_ref, total_ref):
    step = pl.program_id(0)

    @pl.when(step == 0)
    def _():
        total = p0_ref[...].astype(f32) + p1_ref[...].astype(f32)
        total = total + (p2_ref[...].astype(f32) + p3_ref[...].astype(f32))
        total_ref[...] = total.astype(bf16)

    grad = dot(mem_ref[...], total_ref[...], TN).astype(bf16)
    at = pl.multiple_of(step * 512 + z_ref[0] * 128, 128)
    tokens = total_ref[pl.ds(at, 128), :]
    for i in range(16):
        out_ref[i, 0:16, :] = grad[i * 16 : i * 16 + 16]
        out_ref[i, 16:32, :] = tokens[(i // 2) * 16 : (i // 2) * 16 + 16]


def weight_blocks(z, parts, mem):
    n = mem.shape[0]
    part_spec = pl.BlockSpec((n, LANES), lambda s, z: (0, 0))
    return pl.pallas_call(
        weight_kernel,
        grid_spec=pltpu.PrefetchScalarGridSpec(
            num_scalar_prefetch=1,
            grid=(2,),
            in_specs=[part_spec] * 4 + [pl.BlockSpec((n, 256), lambda s, z: (0, s * 4 + z[0]))],
            out_specs=pl.BlockSpec((16, 32, LANES), lambda s, z: (s, 0, 0)),
            scratch_shapes=[pltpu.VMEM((n, LANES), bf16)],
        ),
        out_shape=jax.ShapeDtypeStruct((32, 32, LANES), bf16),
        compiler_params=params(60, dimension_semantics=("arbitrary",)),
        cost_estimate=pl.CostEstimate(flops=0, bytes_accessed=6 << 20, transcendentals=0),
        name="weight_blocks",
    )(z, *parts, mem)


def finish_kernel(dp_ref, in_ref, wk_ref, wv_ref, mg_ref, wkg_ref, wvg_ref, acc_ref):
    p = pl.program_id(0)
    grads = []
    for i in range(2):
        cols = slice(i * LANES, (i + 1) * LANES)
        rows = [in_ref[4 * i + j, 0:16, :].astype(f32) for j in range(4)]
        wkg_ref[:, cols], wvg_ref[:, cols] = swap_halves(rows[0] + rows[1], rows[2] + rows[3])
        even = in_ref[pl.ds(4 * i + dp_ref[0], 1), 16:32, :][0].astype(f32)
        odd = in_ref[pl.ds(4 * i + 2 + dp_ref[0], 1), 16:32, :][0].astype(f32)
        grads.append(swap_halves(even, odd))
    kg = jnp.concatenate([grads[0][0], grads[1][0]], 1).astype(bf16)
    vg = jnp.concatenate([grads[0][1], grads[1][1]], 1).astype(bf16)
    part = dot(kg, wk_ref[...], NT) + dot(vg, wv_ref[...], NT)

    @pl.when(p == 0)
    def _():
        acc_ref[...] = part

    @pl.when(p > 0)
    def _():
        acc_ref[...] += part

    @pl.when(p == pl.num_programs(0) - 1)
    def _():
        mg_ref[0] = acc_ref[...].astype(bf16)


def finish(dp, x, wk, wv):
    d = wk.shape[0]
    w_spec = pl.BlockSpec((d, 256), lambda p, dp: (0, p))
    out_spec = pl.BlockSpec((16, 256), lambda p, dp: (0, p))
    shape = jax.ShapeDtypeStruct((16, wk.shape[1]), f32)
    return pl.pallas_call(
        finish_kernel,
        grid_spec=pltpu.PrefetchScalarGridSpec(
            num_scalar_prefetch=1,
            grid=(4,),
            in_specs=[pl.BlockSpec((8, 32, LANES), lambda p, dp: (p, 0, 0)), w_spec, w_spec],
            out_specs=[pl.BlockSpec((1, 16, d), lambda p, dp: (0, 0, 0)), out_spec, out_spec],
            scratch_shapes=[pltpu.VMEM((16, d), f32)],
        ),
        out_shape=[jax.ShapeDtypeStruct((1, 16, d), bf16), shape, shape],
        compiler_params=params(dimension_semantics=("arbitrary",)),
        cost_estimate=pl.CostEstimate(flops=0, bytes_accessed=12 << 20, transcendentals=0),
        name="finish",
    )(dp, x, wk, wv)


def exchange(x, axes):
    return lax.all_to_all(x, axes, 0, 0, tiled=True)


def shifted(x, axis, k):
    n = lax.axis_size(axis)
    return lax.ppermute(x, axis, [(i, (i + k) % n) for i in range(n)])


def body(q, g, mem, wk, wv, target_modality, memory_modality, allow_pairs):
    z = lax.axis_index("z").reshape(1)
    dp = lax.axis_index("dp").reshape(1)
    mems = [mem] + [shifted(mem, "z", k) for k in (1, 2, 3)]

    labels = jnp.arange(allow_pairs.shape[0], dtype=jnp.int32)
    q_onehot = (target_modality[0][:, None] == labels[None, :]).astype(f32)
    k_onehot = (memory_modality[0][:, None] == labels[None, :]).astype(f32)
    allowed = jnp.dot(jnp.dot(q_onehot, allow_pairs.astype(f32)), k_onehot.T) > 0.5
    allowed = allowed | (jnp.arange(allowed.shape[1], dtype=jnp.int32) == 0)[None, :]
    hide = jnp.where(allowed, 0.0, 1e30).astype(bf16).reshape(32, 1)
    hide = jnp.broadcast_to(hide, (32, LANES))

    payload = project(z, mems, wk, wv, pack_targets(q, g, hide))
    targets = exchange(payload, HEAD_AXES)
    memory = lax.all_gather(mem[0], SAMPLE_AXES, axis=0, tiled=True)

    q_grad, part = attend(targets)
    q_grad = exchange(q_grad, HEAD_AXES)
    parts = [part] + [shifted(part, "z", k) for k in (1, 3, 2)]
    blocks = weight_blocks(z, parts, memory)
    blocks, q_grad = lax.optimization_barrier((blocks, q_grad))
    blocks = exchange(blocks, ("sec", "y", "core", "dp"))
    m_grad, wk_grad, wv_grad = finish(dp, blocks, wk, wv)
    return unpack_targets(q_grad), m_grad, wk_grad, wv_grad


def solution(mesh):
    fine = Mesh(mesh.devices.reshape(2, 4, 4, 2, 2), ALL_AXES)
    rows = P("dp", SAMPLE_AXES, None)
    in_specs = (rows, rows, rows, P(), P(), P("dp", SAMPLE_AXES), P("dp", None), P())
    out_specs = (rows, rows, P(ALL_AXES, None), P(ALL_AXES, None))
    return jax.shard_map(body, mesh=fine, in_specs=in_specs, out_specs=out_specs, check_vma=False)
```

```python
import functools

import jax
import jax.numpy as jnp
from jax import lax
from jax.experimental import pallas as pl
from jax.experimental.pallas import tpu as pltpu
from jax.sharding import Mesh, PartitionSpec as P

HD = 64
BLOCK = 128
LANES = 128
SCALE = 0.125
CHUNK = 256
STEP = 4
NT = (((1,), (1,)), ((), ()))
NN = (((1,), (0,)), ((), ()))
TN = (((0,), (0,)), ((), ()))
HEAD_AXES = ("sec", "y", "core")
SAMPLE_AXES = ("sec", "z", "y", "core")
ALL_AXES = ("sec", "z", "y", "core", "dp")
bf16 = jnp.bfloat16
f32 = jnp.float32


def dot(a, b, dims):
    return lax.dot_general(a, b, dims, preferred_element_type=f32)


def low_half():
    return lax.broadcasted_iota(jnp.int32, (1, LANES), 1) < HD


def swap_halves(a, b):
    lo = low_half()
    return jnp.where(lo, a, pltpu.roll(b, HD, 1)), jnp.where(lo, pltpu.roll(a, HD, 1), b)


def params(mib=48, **kw):
    return pltpu.CompilerParams(vmem_limit_bytes=mib << 20, **kw)


ROWS = (336, 272)
KV_ROW = 256


def pack_kernel(q_ref, g_ref, hide_ref, *out_refs):
    for t, out_ref in enumerate(out_refs):
        for i in range(2):
            cols = slice(i * LANES, (i + 1) * LANES)
            for k, ref in enumerate((q_ref, g_ref)):
                a = ref[0, t * 256 : t * 256 + 128, cols].astype(f32)
                b = ref[0, t * 256 + 128 : t * 256 + 256, cols].astype(f32)
                even, odd = swap_halves(a, b)
                out_ref[2 * i, k * 128 : k * 128 + 128, :] = even.astype(bf16)
                out_ref[2 * i + 1, k * 128 : k * 128 + 128, :] = odd.astype(bf16)
        for i in range(4):
            if t == 0:
                out_ref[i, KV_ROW : KV_ROW + 64, :] = jnp.zeros((64, LANES), bf16)
            out_ref[i, ROWS[t] - 16 : ROWS[t], :] = hide_ref[t * 16 : t * 16 + 16, :]


def pack_targets(q, g, hide):
    return pl.pallas_call(
        pack_kernel,
        grid=(4,),
        in_specs=[
            pl.BlockSpec((1, 512, 256), lambda p: (0, 0, p)),
            pl.BlockSpec((1, 512, 256), lambda p: (0, 0, p)),
            pl.BlockSpec((32, LANES), lambda p: (0, 0)),
        ],
        out_specs=[pl.BlockSpec((4, rows, LANES), lambda p: (p, 0, 0)) for rows in ROWS],
        out_shape=[jax.ShapeDtypeStruct((16, rows, LANES), bf16) for rows in ROWS],
        compiler_params=params(),
        cost_estimate=pl.CostEstimate(flops=0, bytes_accessed=9 << 20, transcendentals=0),
        name="pack_targets",
    )(q, g, hide)


def project_kernel(z_ref, m0_ref, m1_ref, m2_ref, m3_ref, wk_ref, wv_ref, _, out_ref):
    mem = jnp.concatenate([m0_ref[0], m1_ref[0], m2_ref[0], m3_ref[0]], 0)
    k = dot(mem, wk_ref[...], NN)
    v = dot(mem, wv_ref[...], NN)
    for i in range(4):
        cols = slice(i * LANES, (i + 1) * LANES)
        even, odd = swap_halves(k[:, cols], v[:, cols])
        for j in range(4):
            at = pl.multiple_of(lax.rem(z_ref[0] + 4 - j, 4) * 16, 16)
            out_ref[2 * i, pl.ds(at, 16), :] = even[j * 16 : j * 16 + 16].astype(bf16)
            out_ref[2 * i + 1, pl.ds(at, 16), :] = odd[j * 16 : j * 16 + 16].astype(bf16)


def project(z, mems, wk, wv, payload):
    d = wk.shape[0]
    mem_spec = pl.BlockSpec((1, 16, d), lambda p, z: (0, 0, 0))
    w_spec = pl.BlockSpec((d, 512), lambda p, z: (0, p))
    return pl.pallas_call(
        project_kernel,
        grid_spec=pltpu.PrefetchScalarGridSpec(
            num_scalar_prefetch=1,
            grid=(2,),
            in_specs=[mem_spec] * 4 + [w_spec] * 2 + [pl.BlockSpec(memory_space=pl.ANY)],
            out_specs=pl.BlockSpec((8, 64, LANES), lambda p, z: (p, KV_ROW // 64, 0)),
        ),
        out_shape=jax.ShapeDtypeStruct(payload.shape, bf16),
        input_output_aliases={7: 0},
        compiler_params=params(60),
        cost_estimate=pl.CostEstimate(flops=0, bytes_accessed=12 << 20, transcendentals=0),
        name="project",
    )(z, *mems, wk, wv, payload)


def unpack_kernel(first_ref, second_ref, out_ref):
    for t, ref in enumerate((first_ref, second_ref)):
        for i in range(2):
            a, b = swap_halves(ref[2 * i].astype(f32), ref[2 * i + 1].astype(f32))
            cols = slice(i * LANES, (i + 1) * LANES)
            out_ref[0, t * 256 : t * 256 + 128, cols] = a.astype(bf16)
            out_ref[0, t * 256 + 128 : t * 256 + 256, cols] = b.astype(bf16)


def unpack_targets(first, second):
    return pl.pallas_call(
        unpack_kernel,
        grid=(4,),
        in_specs=[pl.BlockSpec((4, LANES, LANES), lambda p: (p, 0, 0))] * 2,
        out_specs=pl.BlockSpec((1, 512, 256), lambda p: (0, 0, p)),
        out_shape=jax.ShapeDtypeStruct((1, 512, 1024), bf16),
        compiler_params=params(),
        cost_estimate=pl.CostEstimate(flops=0, bytes_accessed=6 << 20, transcendentals=0),
        name="unpack_targets",
    )(first, second)


def one_tile(q, g, away, k2_ref, v2_ref, kt_ref, ka_ref, va_ref):
    lo = low_half()
    n = k2_ref.shape[0]
    per = CHUNK // BLOCK
    chunks = n // CHUNK
    rows = [slice(c * CHUNK, c * CHUNK + CHUNK) for c in range(chunks)]
    q = q * jnp.asarray(SCALE, bf16)
    zero = jnp.zeros_like(q)
    q2 = jnp.concatenate([jnp.where(lo, q, zero), jnp.where(lo, zero, q)], 0)
    g2 = jnp.concatenate([jnp.where(lo, g, zero), jnp.where(lo, zero, g)], 0)
    scores = [dot(k2_ref[r, :], q2, NT) for r in rows]
    hidden = []
    top = None
    for j in range(n // BLOCK):
        part = scores[j // per][(j % per) * BLOCK : (j % per + 1) * BLOCK]
        hide = jnp.concatenate([away[j : j + 1], away[8 + j : 9 + j]], 1)
        hidden.append(hide)
        part_top = jnp.max(part, axis=0, keepdims=True) - hide
        top = part_top if top is None else jnp.maximum(top, part_top)
    expd = []
    total = None
    for c in range(chunks):
        parts = [
            jnp.exp(scores[c][i * BLOCK : (i + 1) * BLOCK] - (top + hidden[c * per + i]))
            for i in range(per)
        ]
        e = jnp.concatenate(parts, 0)
        expd.append(e)
        s = jnp.sum(e, axis=0, keepdims=True)
        total = s if total is None else total + s
    inverse = 1.0 / total
    dprobs = []
    delta = None
    for c in range(chunks):
        dp = dot(v2_ref[rows[c], :], g2, NT)
        dprobs.append(dp)
        s = jnp.sum(expd[c] * dp, axis=0, keepdims=True)
        delta = s if delta is None else delta + s
    delta = delta * inverse
    qgt = None
    for c in range(chunks):
        p = expd[c] * inverse
        ds = (p * (dprobs[c] - delta)).astype(bf16)
        va_ref[rows[c], :] += dot(p.astype(bf16), g2, NN)
        ka_ref[rows[c], :] += dot(ds, q2, NN)
        x = dot(kt_ref[:, rows[c]], ds, NN)
        qgt = x if qgt is None else qgt + x
    qgt = qgt * SCALE
    both = jnp.concatenate([qgt[:, :LANES], qgt[:, LANES:]], 0)
    return jnp.transpose(both).astype(bf16)


def attend_kernel(*refs, half):
    if half == 0:
        kv_ref, r_ref, qg_ref, ka_ref, va_ref, k2_ref, v2_ref, kt_ref = refs
    else:
        kv_ref, r_ref, k0_ref, v0_ref, qg_ref, kvg_ref, k2_ref, v2_ref, kt_ref, ka_ref, va_ref = refs
    lo = low_half()

    @pl.when(pl.program_id(0) == 0)
    def _():
        order = [(c, z) for c in (0, 8) for z in range(4)]
        kv = jnp.concatenate(
            [kv_ref[c + i, z * 16 : z * 16 + 16, :] for c, z in order for i in range(8)], 0
        ).astype(f32)
        swapped = pltpu.roll(kv, HD, 1)
        k2 = jnp.where(lo, kv, swapped)
        k2_ref[...] = k2.astype(bf16)
        v2_ref[...] = jnp.where(lo, swapped, kv).astype(bf16)
        kt_ref[...] = jnp.transpose(k2)[:HD].astype(bf16)
        ka_ref[...] = jnp.zeros_like(ka_ref) if half == 0 else k0_ref[...]
        va_ref[...] = jnp.zeros_like(va_ref) if half == 0 else v0_ref[...]

    for i in range(r_ref.shape[0]):
        away = r_ref[i, ROWS[half] - 16 : ROWS[half], :].astype(f32)
        q = r_ref[i, 0:128, :]
        g = r_ref[i, 128:256, :]
        qg_ref[i] = one_tile(q, g, away, k2_ref, v2_ref, kt_ref, ka_ref, va_ref)

    if half == 1:

        @pl.when(pl.program_id(0) == pl.num_programs(0) - 1)
        def _():
            ka = ka_ref[...]
            va = va_ref[...]
            ka = ka + pltpu.roll(ka, HD, 1)
            va = va + pltpu.roll(va, HD, 1)
            kvg_ref[...] = jnp.where(lo, ka, va).astype(bf16)


def attend(half, kv, r, *sums):
    sources = r.shape[0]
    n = 64 * sources
    whole = pl.BlockSpec((n, LANES), lambda i: (0, 0))
    wide = jax.ShapeDtypeStruct((n, LANES), f32)
    kept = [pltpu.VMEM((n, LANES), bf16), pltpu.VMEM((n, LANES), bf16), pltpu.VMEM((HD, n), bf16)]
    held = [pltpu.VMEM((n, LANES), f32), pltpu.VMEM((n, LANES), f32)]
    return pl.pallas_call(
        functools.partial(attend_kernel, half=half),
        grid=(sources // STEP,),
        in_specs=[
            pl.BlockSpec((sources, 64, LANES), lambda i: (0, KV_ROW // 64, 0)),
            pl.BlockSpec((STEP, ROWS[half], LANES), lambda i: (i, 0, 0)),
        ]
        + [whole] * len(sums),
        out_specs=[pl.BlockSpec((STEP, LANES, LANES), lambda i: (i, 0, 0))]
        + ([whole, whole] if half == 0 else [whole]),
        scratch_shapes=kept + ([] if half == 0 else held),
        out_shape=[jax.ShapeDtypeStruct((sources, LANES, LANES), bf16)]
        + ([wide, wide] if half == 0 else [jax.ShapeDtypeStruct((n, LANES), bf16)]),
        compiler_params=params(dimension_semantics=("arbitrary",)),
        cost_estimate=pl.CostEstimate(
            flops=22_000_000_000, bytes_accessed=2 << 20, transcendentals=0
        ),
        name="attend",
    )(kv, r, *sums)


def weight_kernel(z_ref, p0_ref, p1_ref, p2_ref, p3_ref, mem_ref, out_ref, total_ref):
    step = pl.program_id(0)

    @pl.when(step == 0)
    def _():
        total = p0_ref[...].astype(f32) + p1_ref[...].astype(f32)
        total = total + (p2_ref[...].astype(f32) + p3_ref[...].astype(f32))
        total_ref[...] = total.astype(bf16)

    grad = dot(mem_ref[...], total_ref[...], TN).astype(bf16)
    at = pl.multiple_of(step * 512 + z_ref[0] * 128, 128)
    tokens = total_ref[pl.ds(at, 128), :]
    for i in range(16):
        out_ref[i, 0:16, :] = grad[i * 16 : i * 16 + 16]
        out_ref[i, 16:32, :] = tokens[(i // 2) * 16 : (i // 2) * 16 + 16]


def weight_blocks(z, parts, mem):
    n = mem.shape[0]
    part_spec = pl.BlockSpec((n, LANES), lambda s, z: (0, 0))
    return pl.pallas_call(
        weight_kernel,
        grid_spec=pltpu.PrefetchScalarGridSpec(
            num_scalar_prefetch=1,
            grid=(2,),
            in_specs=[part_spec] * 4 + [pl.BlockSpec((n, 256), lambda s, z: (0, s * 4 + z[0]))],
            out_specs=pl.BlockSpec((16, 32, LANES), lambda s, z: (s, 0, 0)),
            scratch_shapes=[pltpu.VMEM((n, LANES), bf16)],
        ),
        out_shape=jax.ShapeDtypeStruct((32, 32, LANES), bf16),
        compiler_params=params(60, dimension_semantics=("arbitrary",)),
        cost_estimate=pl.CostEstimate(flops=0, bytes_accessed=6 << 20, transcendentals=0),
        name="weight_blocks",
    )(z, *parts, mem)


def finish_kernel(dp_ref, in_ref, wk_ref, wv_ref, mg_ref, wkg_ref, wvg_ref, acc_ref):
    p = pl.program_id(0)
    grads = []
    for i in range(4):
        cols = slice(i * LANES, (i + 1) * LANES)
        rows = [in_ref[4 * i + j, 0:16, :].astype(f32) for j in range(4)]
        wkg_ref[:, cols], wvg_ref[:, cols] = swap_halves(rows[0] + rows[1], rows[2] + rows[3])
        even = in_ref[pl.ds(4 * i + dp_ref[0], 1), 16:32, :][0].astype(f32)
        odd = in_ref[pl.ds(4 * i + 2 + dp_ref[0], 1), 16:32, :][0].astype(f32)
        grads.append(swap_halves(even, odd))
    kg = jnp.concatenate([x[0] for x in grads], 1).astype(bf16)
    vg = jnp.concatenate([x[1] for x in grads], 1).astype(bf16)
    part = dot(kg, wk_ref[...], NT) + dot(vg, wv_ref[...], NT)

    @pl.when(p == 0)
    def _():
        acc_ref[...] = part

    @pl.when(p > 0)
    def _():
        acc_ref[...] += part

    @pl.when(p == pl.num_programs(0) - 1)
    def _():
        mg_ref[0] = acc_ref[...].astype(bf16)


def finish(dp, x, wk, wv):
    d = wk.shape[0]
    w_spec = pl.BlockSpec((d, 512), lambda p, dp: (0, p))
    out_spec = pl.BlockSpec((16, 512), lambda p, dp: (0, p))
    shape = jax.ShapeDtypeStruct((16, wk.shape[1]), f32)
    return pl.pallas_call(
        finish_kernel,
        grid_spec=pltpu.PrefetchScalarGridSpec(
            num_scalar_prefetch=1,
            grid=(2,),
            in_specs=[pl.BlockSpec((16, 32, LANES), lambda p, dp: (p, 0, 0)), w_spec, w_spec],
            out_specs=[pl.BlockSpec((1, 16, d), lambda p, dp: (0, 0, 0)), out_spec, out_spec],
            scratch_shapes=[pltpu.VMEM((16, d), f32)],
        ),
        out_shape=[jax.ShapeDtypeStruct((1, 16, d), bf16), shape, shape],
        compiler_params=params(60, dimension_semantics=("arbitrary",)),
        cost_estimate=pl.CostEstimate(flops=0, bytes_accessed=12 << 20, transcendentals=0),
        name="finish",
    )(dp, x, wk, wv)


def exchange(x, axes):
    return lax.all_to_all(x, axes, 0, 0, tiled=True)


def shifted(x, axis, k):
    n = lax.axis_size(axis)
    return lax.ppermute(x, axis, [(i, (i + k) % n) for i in range(n)])


def body(q, g, mem, wk, wv, target_modality, memory_modality, allow_pairs):
    z = lax.axis_index("z").reshape(1)
    dp = lax.axis_index("dp").reshape(1)
    mems = [mem] + [shifted(mem, "z", k) for k in (1, 2, 3)]

    labels = jnp.arange(allow_pairs.shape[0], dtype=jnp.int32)
    q_onehot = (target_modality[0][:, None] == labels[None, :]).astype(f32)
    k_onehot = (memory_modality[0][:, None] == labels[None, :]).astype(f32)
    allowed = jnp.dot(jnp.dot(q_onehot, allow_pairs.astype(f32)), k_onehot.T) > 0.5
    allowed = allowed | (jnp.arange(allowed.shape[1], dtype=jnp.int32) == 0)[None, :]
    hide = jnp.where(allowed, 0.0, 1e30).astype(bf16).reshape(32, 1)
    hide = jnp.broadcast_to(hide, (32, LANES))

    first, second = pack_targets(q, g, hide)
    first = exchange(project(z, mems, wk, wv, first), HEAD_AXES)
    memory = lax.all_gather(mem[0], SAMPLE_AXES, axis=0, tiled=True)
    first, second = lax.optimization_barrier((first, second))
    second = exchange(second, HEAD_AXES)

    q_first, k_sum, v_sum = attend(0, first, first)
    q_first = exchange(q_first, HEAD_AXES)
    q_second, part = attend(1, first, second, k_sum, v_sum)
    q_second = exchange(q_second, HEAD_AXES)
    parts = [part] + [shifted(part, "z", k) for k in (1, 3, 2)]
    blocks = weight_blocks(z, parts, memory)
    blocks, q_second = lax.optimization_barrier((blocks, q_second))
    blocks = exchange(blocks, ("sec", "y", "core", "dp"))
    m_grad, wk_grad, wv_grad = finish(dp, blocks, wk, wv)
    return unpack_targets(q_first, q_second), m_grad, wk_grad, wv_grad


def solution(mesh):
    fine = Mesh(mesh.devices.reshape(2, 4, 4, 2, 2), ALL_AXES)
    rows = P("dp", SAMPLE_AXES, None)
    in_specs = (rows, rows, rows, P(), P(), P("dp", SAMPLE_AXES), P("dp", None), P())
    out_specs = (rows, rows, P(ALL_AXES, None), P(ALL_AXES, None))
    return jax.shard_map(body, mesh=fine, in_specs=in_specs, out_specs=out_specs, check_vma=False)
```

```python
import functools

import jax
import jax.numpy as jnp
from jax import lax
from jax.experimental import pallas as pl
from jax.experimental.pallas import tpu as pltpu
from jax.sharding import Mesh, PartitionSpec as P

HD = 64
BLOCK = 128
LANES = 128
SCALE = 0.125
CHUNK = 256
NT = (((1,), (1,)), ((), ()))
NN = (((1,), (0,)), ((), ()))
TN = (((0,), (0,)), ((), ()))
HEAD_AXES = ("sec", "y", "core")
SAMPLE_AXES = ("sec", "z", "y", "core")
ALL_AXES = ("sec", "z", "y", "core", "dp")
bf16 = jnp.bfloat16
f32 = jnp.float32


def dot(a, b, dims):
    return lax.dot_general(a, b, dims, preferred_element_type=f32)


def low_half():
    return lax.broadcasted_iota(jnp.int32, (1, LANES), 1) < HD


def swap_halves(a, b):
    lo = low_half()
    return jnp.where(lo, a, pltpu.roll(b, HD, 1)), jnp.where(lo, pltpu.roll(a, HD, 1), b)


def params(mib=48, **kw):
    return pltpu.CompilerParams(vmem_limit_bytes=mib << 20, **kw)


ROWS = 592
KV_ROW = 512
MASK_ROW = 576


def prepare_kernel(z_ref, q_ref, g_ref, hide_ref, m0_ref, m1_ref, m2_ref, m3_ref, wk_ref, wv_ref, out_ref):
    mem = jnp.concatenate([m0_ref[0], m1_ref[0], m2_ref[0], m3_ref[0]], 0)
    keys = dot(mem, wk_ref[...], NN)
    values = dot(mem, wv_ref[...], NN)
    for i in range(2):
        cols = slice(i * LANES, (i + 1) * LANES)
        for k, ref in enumerate((q_ref, g_ref)):
            for t in range(2):
                a = ref[0, t * 256 : t * 256 + 128, cols].astype(f32)
                b = ref[0, t * 256 + 128 : t * 256 + 256, cols].astype(f32)
                even, odd = swap_halves(a, b)
                rows = slice(k * 256 + t * 128, k * 256 + t * 128 + 128)
                out_ref[2 * i, rows, :] = even.astype(bf16)
                out_ref[2 * i + 1, rows, :] = odd.astype(bf16)
        for n, x in enumerate(swap_halves(keys[:, cols], values[:, cols])):
            x = x.astype(bf16)
            for j in range(4):
                at = pl.multiple_of(KV_ROW + lax.rem(z_ref[0] + 4 - j, 4) * 16, 16)
                out_ref[2 * i + n, pl.ds(at, 16), :] = x[j * 16 : j * 16 + 16]
            out_ref[2 * i + n, MASK_ROW : MASK_ROW + 16, :] = hide_ref[...]


def prepare(z, q, g, hide, mems, wk, wv):
    d = wk.shape[0]
    target_spec = pl.BlockSpec((1, 512, 256), lambda p, z: (0, 0, p))
    mem_spec = pl.BlockSpec((1, 16, d), lambda p, z: (0, 0, 0))
    w_spec = pl.BlockSpec((d, 256), lambda p, z: (0, p))
    return pl.pallas_call(
        prepare_kernel,
        grid_spec=pltpu.PrefetchScalarGridSpec(
            num_scalar_prefetch=1,
            grid=(4,),
            in_specs=[target_spec] * 2
            + [pl.BlockSpec((16, LANES), lambda p, z: (0, 0))]
            + [mem_spec] * 4
            + [w_spec] * 2,
            out_specs=pl.BlockSpec((4, ROWS, LANES), lambda p, z: (p, 0, 0)),
        ),
        out_shape=jax.ShapeDtypeStruct((16, ROWS, LANES), bf16),
        compiler_params=params(60),
        cost_estimate=pl.CostEstimate(flops=0, bytes_accessed=16 << 20, transcendentals=0),
        name="prepare",
    )(z, q, g, hide, *mems, wk, wv)


def unpack_kernel(in_ref, out_ref):
    for i in range(2):
        for t in range(2):
            even = in_ref[2 * i, t * 128 : t * 128 + 128, :].astype(f32)
            odd = in_ref[2 * i + 1, t * 128 : t * 128 + 128, :].astype(f32)
            a, b = swap_halves(even, odd)
            cols = slice(i * LANES, (i + 1) * LANES)
            out_ref[0, t * 256 : t * 256 + 128, cols] = a.astype(bf16)
            out_ref[0, t * 256 + 128 : t * 256 + 256, cols] = b.astype(bf16)


def unpack_targets(x):
    return pl.pallas_call(
        unpack_kernel,
        grid=(4,),
        in_specs=[pl.BlockSpec((4, 256, LANES), lambda p: (p, 0, 0))],
        out_specs=pl.BlockSpec((1, 512, 256), lambda p: (0, 0, p)),
        out_shape=jax.ShapeDtypeStruct((1, 512, 1024), bf16),
        compiler_params=params(),
        cost_estimate=pl.CostEstimate(flops=0, bytes_accessed=6 << 20, transcendentals=0),
        name="unpack_targets",
    )(x)


def one_tile(q, g, away, k2_ref, v2_ref, kt_ref, ka_ref, va_ref):
    lo = low_half()
    n = k2_ref.shape[0]
    per = CHUNK // BLOCK
    chunks = n // CHUNK
    rows = [slice(c * CHUNK, c * CHUNK + CHUNK) for c in range(chunks)]
    q = q * jnp.asarray(SCALE, bf16)
    zero = jnp.zeros_like(q)
    q2 = jnp.concatenate([jnp.where(lo, q, zero), jnp.where(lo, zero, q)], 0)
    g2 = jnp.concatenate([jnp.where(lo, g, zero), jnp.where(lo, zero, g)], 0)
    scores = [dot(k2_ref[r, :], q2, NT) for r in rows]
    other = pltpu.roll(away, HD, 1)
    away = (jnp.where(lo, away, other), jnp.where(lo, other, away))
    hidden = []
    top = None
    for j in range(n // BLOCK):
        part = scores[j // per][(j % per) * BLOCK : (j % per + 1) * BLOCK]
        at = j // 2
        hide = jnp.concatenate([away[j % 2][at : at + 1], away[j % 2][4 + at : 5 + at]], 1)
        hidden.append(hide)
        part_top = jnp.max(part, axis=0, keepdims=True) - hide
        top = part_top if top is None else jnp.maximum(top, part_top)
    expd = []
    total = None
    for c in range(chunks):
        parts = [
            jnp.exp(scores[c][i * BLOCK : (i + 1) * BLOCK] - (top + hidden[c * per + i]))
            for i in range(per)
        ]
        e = jnp.concatenate(parts, 0)
        expd.append(e)
        s = jnp.sum(e, axis=0, keepdims=True)
        total = s if total is None else total + s
    inverse = 1.0 / total
    dprobs = []
    delta = None
    for c in range(chunks):
        dp = dot(v2_ref[rows[c], :], g2, NT)
        dprobs.append(dp)
        s = jnp.sum(expd[c] * dp, axis=0, keepdims=True)
        delta = s if delta is None else delta + s
    delta = delta * inverse
    qgt = None
    for c in range(chunks):
        p = expd[c] * inverse
        ds = (p * (dprobs[c] - delta)).astype(bf16)
        va_ref[rows[c], :] += dot(p.astype(bf16), g2, NN)
        ka_ref[rows[c], :] += dot(ds, q2, NN)
        x = dot(kt_ref[:, rows[c]], ds, NN)
        qgt = x if qgt is None else qgt + x
    qgt = qgt * SCALE
    both = jnp.concatenate([qgt[:, :LANES], qgt[:, LANES:]], 0)
    return jnp.transpose(both).astype(bf16)


def attend_kernel(kv_ref, r_ref, qg_ref, kvg_ref, k2_ref, v2_ref, kt_ref, ka_ref, va_ref):
    lo = low_half()
    step = pl.program_id(0)

    @pl.when(step == 0)
    def _():
        order = [(c, z) for c in (0, 8) for z in range(4)]
        kv = jnp.concatenate(
            [kv_ref[c + i, z * 16 : z * 16 + 16, :] for c, z in order for i in range(8)], 0
        ).astype(f32)
        swapped = pltpu.roll(kv, HD, 1)
        k2 = jnp.where(lo, kv, swapped)
        k2_ref[...] = k2.astype(bf16)
        v2_ref[...] = jnp.where(lo, swapped, kv).astype(bf16)
        kt_ref[...] = jnp.transpose(k2)[:HD].astype(bf16)
        ka_ref[...] = jnp.zeros_like(ka_ref)
        va_ref[...] = jnp.zeros_like(va_ref)

    for i in range(r_ref.shape[0]):
        for t in range(2):
            away = r_ref[i, MASK_ROW : MASK_ROW + 16, :].astype(f32)[t * 8 : t * 8 + 8]
            q = r_ref[i, t * 128 : t * 128 + 128, :]
            g = r_ref[i, 256 + t * 128 : 384 + t * 128, :]
            qg_ref[i, t * 128 : t * 128 + 128, :] = one_tile(
                q, g, away, k2_ref, v2_ref, kt_ref, ka_ref, va_ref
            )

    @pl.when(step == pl.num_programs(0) - 1)
    def _():
        ka = ka_ref[...]
        va = va_ref[...]
        ka = ka + pltpu.roll(ka, HD, 1)
        va = va + pltpu.roll(va, HD, 1)
        kvg_ref[...] = jnp.where(lo, ka, va).astype(bf16)


def attend(r):
    sources = r.shape[0]
    n = 64 * sources
    return pl.pallas_call(
        attend_kernel,
        grid=(sources // 2,),
        in_specs=[
            pl.BlockSpec((sources, 64, LANES), lambda i: (0, KV_ROW // 64, 0)),
            pl.BlockSpec((2, ROWS, LANES), lambda i: (i, 0, 0)),
        ],
        out_specs=[
            pl.BlockSpec((2, 256, LANES), lambda i: (i, 0, 0)),
            pl.BlockSpec((n, LANES), lambda i: (0, 0)),
        ],
        scratch_shapes=[
            pltpu.VMEM((n, LANES), bf16),
            pltpu.VMEM((n, LANES), bf16),
            pltpu.VMEM((HD, n), bf16),
            pltpu.VMEM((n, LANES), f32),
            pltpu.VMEM((n, LANES), f32),
        ],
        out_shape=[
            jax.ShapeDtypeStruct((sources, 256, LANES), bf16),
            jax.ShapeDtypeStruct((n, LANES), bf16),
        ],
        compiler_params=params(dimension_semantics=("arbitrary",)),
        cost_estimate=pl.CostEstimate(
            flops=40_000_000_000, bytes_accessed=4 << 20, transcendentals=0
        ),
        name="attend",
    )(r, r)


def spread_kernel(z_ref, m0_ref, m1_ref, m2_ref, m3_ref, out_ref):
    mem = jnp.concatenate([m0_ref[0], m1_ref[0], m2_ref[0], m3_ref[0]], 0)
    for i in range(16):
        out_ref[i] = mem


def spread(z, mems):
    return pl.pallas_call(
        spread_kernel,
        grid_spec=pltpu.PrefetchScalarGridSpec(
            num_scalar_prefetch=1,
            grid=(2,),
            in_specs=[pl.BlockSpec((1, 16, 256), lambda s, z: (0, 0, s * 4 + z[0]))] * 4,
            out_specs=pl.BlockSpec((16, 64, 256), lambda s, z: (0, 0, s)),
        ),
        out_shape=jax.ShapeDtypeStruct((16, 64, 512), bf16),
        compiler_params=params(),
        cost_estimate=pl.CostEstimate(flops=0, bytes_accessed=1 << 20, transcendentals=0),
        name="spread",
    )(z, *mems)


def weight_kernel(z_ref, p0_ref, p1_ref, p2_ref, p3_ref, mem_ref, out_ref, total_ref, moved_ref):
    step = pl.program_id(0)

    @pl.when(step == 0)
    def _():
        total = p0_ref[...].astype(f32) + p1_ref[...].astype(f32)
        total = total + (p2_ref[...].astype(f32) + p3_ref[...].astype(f32))
        total_ref[...] = total.astype(bf16)
        for i in range(16):
            for j in range(4):
                at = (i // 8) * 512 + lax.rem(z_ref[0] + 4 - j, 4) * 128 + (i % 8) * 16
                rows = slice(i * 64 + j * 16, i * 64 + j * 16 + 16)
                moved_ref[rows, :] = total_ref[pl.ds(pl.multiple_of(at, 16), 16), :]

    grad = dot(mem_ref[...], moved_ref[...], TN).astype(bf16)
    at = pl.multiple_of(step * 512 + z_ref[0] * 128, 128)
    tokens = total_ref[pl.ds(at, 128), :]
    for i in range(16):
        out_ref[i, 0:16, :] = grad[i * 16 : i * 16 + 16]
        out_ref[i, 16:32, :] = tokens[(i // 2) * 16 : (i // 2) * 16 + 16]


def weight_blocks(z, parts, mem):
    n = mem.shape[0]
    part_spec = pl.BlockSpec((n, LANES), lambda s, z: (0, 0))
    return pl.pallas_call(
        weight_kernel,
        grid_spec=pltpu.PrefetchScalarGridSpec(
            num_scalar_prefetch=1,
            grid=(2,),
            in_specs=[part_spec] * 4 + [pl.BlockSpec((n, 256), lambda s, z: (0, s))],
            out_specs=pl.BlockSpec((16, 32, LANES), lambda s, z: (s, 0, 0)),
            scratch_shapes=[pltpu.VMEM((n, LANES), bf16), pltpu.VMEM((n, LANES), bf16)],
        ),
        out_shape=jax.ShapeDtypeStruct((32, 32, LANES), bf16),
        compiler_params=params(dimension_semantics=("arbitrary",)),
        cost_estimate=pl.CostEstimate(flops=0, bytes_accessed=6 << 20, transcendentals=0),
        name="weight_blocks",
    )(z, *parts, mem)


def finish_kernel(dp_ref, in_ref, wk_ref, wv_ref, mg_ref, wkg_ref, wvg_ref, acc_ref):
    p = pl.program_id(0)
    grads = []
    for i in range(4):
        cols = slice(i * LANES, (i + 1) * LANES)
        rows = [in_ref[4 * i + j, 0:16, :].astype(f32) for j in range(4)]
        wkg_ref[:, cols], wvg_ref[:, cols] = swap_halves(rows[0] + rows[1], rows[2] + rows[3])
        even = in_ref[pl.ds(4 * i + dp_ref[0], 1), 16:32, :][0].astype(f32)
        odd = in_ref[pl.ds(4 * i + 2 + dp_ref[0], 1), 16:32, :][0].astype(f32)
        grads.append(swap_halves(even, odd))
    kg = jnp.concatenate([x[0] for x in grads], 1).astype(bf16)
    vg = jnp.concatenate([x[1] for x in grads], 1).astype(bf16)
    part = dot(kg, wk_ref[...], NT) + dot(vg, wv_ref[...], NT)

    @pl.when(p == 0)
    def _():
        acc_ref[...] = part

    @pl.when(p > 0)
    def _():
        acc_ref[...] += part

    @pl.when(p == pl.num_programs(0) - 1)
    def _():
        mg_ref[0] = acc_ref[...].astype(bf16)


def finish(dp, x, wk, wv):
    d = wk.shape[0]
    w_spec = pl.BlockSpec((d, 512), lambda p, dp: (0, p))
    out_spec = pl.BlockSpec((16, 512), lambda p, dp: (0, p))
    shape = jax.ShapeDtypeStruct((16, wk.shape[1]), f32)
    return pl.pallas_call(
        finish_kernel,
        grid_spec=pltpu.PrefetchScalarGridSpec(
            num_scalar_prefetch=1,
            grid=(2,),
            in_specs=[pl.BlockSpec((16, 32, LANES), lambda p, dp: (p, 0, 0)), w_spec, w_spec],
            out_specs=[pl.BlockSpec((1, 16, d), lambda p, dp: (0, 0, 0)), out_spec, out_spec],
            scratch_shapes=[pltpu.VMEM((16, d), f32)],
        ),
        out_shape=[jax.ShapeDtypeStruct((1, 16, d), bf16), shape, shape],
        compiler_params=params(60, dimension_semantics=("arbitrary",)),
        cost_estimate=pl.CostEstimate(flops=0, bytes_accessed=12 << 20, transcendentals=0),
        name="finish",
    )(dp, x, wk, wv)


def exchange(x, axes):
    return lax.all_to_all(x, axes, 0, 0, tiled=True)


def shifted(x, axis, k):
    n = lax.axis_size(axis)
    return lax.ppermute(x, axis, [(i, (i + k) % n) for i in range(n)])


def body(q, g, mem, wk, wv, target_modality, memory_modality, allow_pairs):
    z = lax.axis_index("z").reshape(1)
    dp = lax.axis_index("dp").reshape(1)
    mems = [mem] + [shifted(mem, "z", k) for k in (1, 2, 3)]

    labels = jnp.arange(allow_pairs.shape[0], dtype=jnp.int32)
    q_onehot = (target_modality[0][:, None] == labels[None, :]).astype(f32)
    k_onehot = (memory_modality[0][:, None] == labels[None, :]).astype(f32)
    allowed = jnp.dot(jnp.dot(q_onehot, allow_pairs.astype(f32)), k_onehot.T) > 0.5
    allowed = allowed | (jnp.arange(allowed.shape[1], dtype=jnp.int32) == 0)[None, :]
    hide = jnp.where(allowed, 0.0, 1e30).astype(bf16).reshape(16, 2, 1)
    hide = jnp.broadcast_to(hide, (16, 2, HD)).reshape(16, LANES)

    payload = prepare(z, q, g, hide, mems, wk, wv)
    payload, mems = lax.optimization_barrier((payload, mems))
    columns = spread(z, mems)
    targets = exchange(payload, HEAD_AXES)
    columns, targets = lax.optimization_barrier((columns, targets))
    memory = exchange(columns, HEAD_AXES).reshape(1024, 512)

    q_grad, part = attend(targets)
    part, memory = lax.optimization_barrier((part, memory))
    q_grad = exchange(q_grad, HEAD_AXES)
    parts = [part] + [shifted(part, "z", k) for k in (1, 3, 2)]
    blocks = weight_blocks(z, parts, memory)
    blocks, q_grad = lax.optimization_barrier((blocks, q_grad))
    blocks = exchange(blocks, ("sec", "y", "core", "dp"))
    m_grad, wk_grad, wv_grad = finish(dp, blocks, wk, wv)
    return unpack_targets(q_grad), m_grad, wk_grad, wv_grad


def solution(mesh):
    fine = Mesh(mesh.devices.reshape(2, 4, 4, 2, 2), ALL_AXES)
    rows = P("dp", SAMPLE_AXES, None)
    in_specs = (rows, rows, rows, P(), P(), P("dp", SAMPLE_AXES), P("dp", None), P())
    out_specs = (rows, rows, P(ALL_AXES, None), P(ALL_AXES, None))
    return jax.shard_map(body, mesh=fine, in_specs=in_specs, out_specs=out_specs, check_vma=False)
```

```python
import functools

import jax
import jax.numpy as jnp
from jax import lax
from jax.experimental import pallas as pl
from jax.experimental.pallas import tpu as pltpu
from jax.sharding import Mesh, PartitionSpec as P

HD = 64
BLOCK = 128
LANES = 128
SCALE = 0.125
CHUNK = 256
NT = (((1,), (1,)), ((), ()))
NN = (((1,), (0,)), ((), ()))
TN = (((0,), (0,)), ((), ()))
HEAD_AXES = ("z", "y")
SUM_AXES = ("sec", "core")
SAMPLE_AXES = ("sec", "z", "y", "core")
ALL_AXES = ("sec", "z", "y", "core", "dp")
bf16 = jnp.bfloat16
f32 = jnp.float32


def dot(a, b, dims):
    return lax.dot_general(a, b, dims, preferred_element_type=f32)


def low_half():
    return lax.broadcasted_iota(jnp.int32, (1, LANES), 1) < HD


def swap_halves(a, b):
    lo = low_half()
    return jnp.where(lo, a, pltpu.roll(b, HD, 1)), jnp.where(lo, pltpu.roll(a, HD, 1), b)


def params(mib=48, **kw):
    return pltpu.CompilerParams(vmem_limit_bytes=mib << 20, **kw)


ROWS = (336, 272)
KV_ROW = 256
STEP = 4


def prepare_kernel(me_ref, q_ref, g_ref, hide_ref, m0_ref, m1_ref, m2_ref, m3_ref, wk_ref, wv_ref, *out_refs):
    mem = jnp.concatenate([m0_ref[0], m1_ref[0], m2_ref[0], m3_ref[0]], 0)
    keys = dot(mem, wk_ref[...], NN)
    values = dot(mem, wv_ref[...], NN)
    for i in range(2):
        cols = slice(i * LANES, (i + 1) * LANES)
        for t, out_ref in enumerate(out_refs):
            for k, ref in enumerate((q_ref, g_ref)):
                a = ref[0, t * 256 : t * 256 + 128, cols].astype(f32)
                b = ref[0, t * 256 + 128 : t * 256 + 256, cols].astype(f32)
                even, odd = swap_halves(a, b)
                out_ref[2 * i, k * 128 : k * 128 + 128, :] = even.astype(bf16)
                out_ref[2 * i + 1, k * 128 : k * 128 + 128, :] = odd.astype(bf16)
            for n in range(2):
                out_ref[2 * i + n, ROWS[t] - 16 : ROWS[t], :] = hide_ref[...]
        for n, x in enumerate(swap_halves(keys[:, cols], values[:, cols])):
            x = x.astype(bf16)
            for j in range(4):
                at = pl.multiple_of(KV_ROW + (me_ref[0] ^ j) * 16, 16)
                out_refs[0][2 * i + n, pl.ds(at, 16), :] = x[j * 16 : j * 16 + 16]


def prepare(me, q, g, hide, mems, wk, wv):
    d = wk.shape[0]
    target_spec = pl.BlockSpec((1, 512, 256), lambda p, me: (0, 0, p))
    mem_spec = pl.BlockSpec((1, 16, d), lambda p, me: (0, 0, 0))
    w_spec = pl.BlockSpec((d, 256), lambda p, me: (0, p))
    return pl.pallas_call(
        prepare_kernel,
        grid_spec=pltpu.PrefetchScalarGridSpec(
            num_scalar_prefetch=1,
            grid=(4,),
            in_specs=[target_spec] * 2
            + [pl.BlockSpec((16, LANES), lambda p, me: (0, 0))]
            + [mem_spec] * 4
            + [w_spec] * 2,
            out_specs=[pl.BlockSpec((4, rows, LANES), lambda p, me: (p, 0, 0)) for rows in ROWS],
        ),
        out_shape=[jax.ShapeDtypeStruct((16, rows, LANES), bf16) for rows in ROWS],
        compiler_params=params(60),
        cost_estimate=pl.CostEstimate(flops=0, bytes_accessed=16 << 20, transcendentals=0),
        name="prepare",
    )(me, q, g, hide, *mems, wk, wv)


def unpack_kernel(in_ref, out_ref):
    for i in range(2):
        for t in range(2):
            even = in_ref[2 * i, t * 128 : t * 128 + 128, :].astype(f32)
            odd = in_ref[2 * i + 1, t * 128 : t * 128 + 128, :].astype(f32)
            a, b = swap_halves(even, odd)
            cols = slice(i * LANES, (i + 1) * LANES)
            out_ref[0, t * 256 : t * 256 + 128, cols] = a.astype(bf16)
            out_ref[0, t * 256 + 128 : t * 256 + 256, cols] = b.astype(bf16)


def unpack_targets(x):
    return pl.pallas_call(
        unpack_kernel,
        grid=(4,),
        in_specs=[pl.BlockSpec((4, 256, LANES), lambda p: (p, 0, 0))],
        out_specs=pl.BlockSpec((1, 512, 256), lambda p: (0, 0, p)),
        out_shape=jax.ShapeDtypeStruct((1, 512, 1024), bf16),
        compiler_params=params(),
        cost_estimate=pl.CostEstimate(flops=0, bytes_accessed=6 << 20, transcendentals=0),
        name="unpack_targets",
    )(x)


def one_tile(q, g, away, k2_ref, v2_ref, kt_ref, ka_ref, va_ref):
    lo = low_half()
    n = k2_ref.shape[0]
    per = CHUNK // BLOCK
    chunks = n // CHUNK
    rows = [slice(c * CHUNK, c * CHUNK + CHUNK) for c in range(chunks)]
    q = q * jnp.asarray(SCALE, bf16)
    zero = jnp.zeros_like(q)
    q2 = jnp.concatenate([jnp.where(lo, q, zero), jnp.where(lo, zero, q)], 0)
    g2 = jnp.concatenate([jnp.where(lo, g, zero), jnp.where(lo, zero, g)], 0)
    scores = [dot(k2_ref[r, :], q2, NT) for r in rows]
    other = pltpu.roll(away, HD, 1)
    away = (jnp.where(lo, away, other), jnp.where(lo, other, away))
    hidden = []
    top = None
    for j in range(n // BLOCK):
        part = scores[j // per][(j % per) * BLOCK : (j % per + 1) * BLOCK]
        at = j // 2
        hide = jnp.concatenate([away[j % 2][at : at + 1], away[j % 2][4 + at : 5 + at]], 1)
        hidden.append(hide)
        part_top = jnp.max(part, axis=0, keepdims=True) - hide
        top = part_top if top is None else jnp.maximum(top, part_top)
    expd = []
    total = None
    for c in range(chunks):
        parts = [
            jnp.exp(scores[c][i * BLOCK : (i + 1) * BLOCK] - (top + hidden[c * per + i]))
            for i in range(per)
        ]
        e = jnp.concatenate(parts, 0)
        expd.append(e)
        s = jnp.sum(e, axis=0, keepdims=True)
        total = s if total is None else total + s
    inverse = 1.0 / total
    dprobs = []
    delta = None
    for c in range(chunks):
        dp = dot(v2_ref[rows[c], :], g2, NT)
        dprobs.append(dp)
        s = jnp.sum(expd[c] * dp, axis=0, keepdims=True)
        delta = s if delta is None else delta + s
    delta = delta * inverse
    qgt = None
    for c in range(chunks):
        p = expd[c] * inverse
        ds = (p * (dprobs[c] - delta)).astype(bf16)
        va_ref[rows[c], :] += dot(p.astype(bf16), g2, NN)
        ka_ref[rows[c], :] += dot(ds, q2, NN)
        x = dot(kt_ref[:, rows[c]], ds, NN)
        qgt = x if qgt is None else qgt + x
    qgt = qgt * SCALE
    both = jnp.concatenate([qgt[:, :LANES], qgt[:, LANES:]], 0)
    return jnp.transpose(both).astype(bf16)


def attend_kernel(*refs, half):
    if half == 0:
        kv_ref, r_ref, qg_ref, kvg_ref, k2_ref, v2_ref, kt_ref, ka_ref, va_ref = refs
    else:
        kv_ref, r_ref, before_ref, _, qg_ref, kvg_ref, k2_ref, v2_ref, kt_ref, ka_ref, va_ref = refs
    lo = low_half()

    @pl.when(pl.program_id(0) == 0)
    def _():
        order = [(i, j * 32) for j in range(2) for i in range(16)]
        kv = jnp.concatenate([kv_ref[i, at : at + 32, :] for i, at in order], 0).astype(f32)
        swapped = pltpu.roll(kv, HD, 1)
        k2 = jnp.where(lo, kv, swapped)
        k2_ref[...] = k2.astype(bf16)
        v2_ref[...] = jnp.where(lo, swapped, kv).astype(bf16)
        kt_ref[...] = jnp.transpose(k2)[:HD].astype(bf16)
        ka_ref[...] = jnp.zeros_like(ka_ref)
        va_ref[...] = jnp.zeros_like(va_ref)

    for i in range(STEP):
        away = r_ref[i, ROWS[half] - 16 : ROWS[half], :].astype(f32)[half * 8 : half * 8 + 8]
        q = r_ref[i, 0:128, :]
        g = r_ref[i, 128:256, :]
        qg_ref[i] = one_tile(q, g, away, k2_ref, v2_ref, kt_ref, ka_ref, va_ref)

    @pl.when(pl.program_id(0) == pl.num_programs(0) - 1)
    def _():
        ka = ka_ref[...]
        va = va_ref[...]
        ka = ka + pltpu.roll(ka, HD, 1)
        va = va + pltpu.roll(va, HD, 1)
        kvg = jnp.where(lo, ka, va)
        if half == 1:
            kvg = kvg + before_ref[...].astype(f32)
        kvg_ref[...] = kvg.astype(bf16)


def attend(half, kv, r, *before):
    sources = r.shape[0]
    n = 64 * sources
    whole = pl.BlockSpec((n, LANES), lambda i: (0, 0))
    return pl.pallas_call(
        functools.partial(attend_kernel, half=half),
        grid=(sources // STEP,),
        in_specs=[
            pl.BlockSpec((sources, 64, LANES), lambda i: (0, KV_ROW // 64, 0)),
            pl.BlockSpec((STEP, ROWS[half], LANES), lambda i: (i, 0, 0)),
        ]
        + ([] if half == 0 else [whole, pl.BlockSpec(memory_space=pl.ANY)]),
        out_specs=[pl.BlockSpec((STEP, LANES, LANES), lambda i: (i, half, 0)), whole],
        scratch_shapes=[
            pltpu.VMEM((n, LANES), bf16),
            pltpu.VMEM((n, LANES), bf16),
            pltpu.VMEM((HD, n), bf16),
            pltpu.VMEM((n, LANES), f32),
            pltpu.VMEM((n, LANES), f32),
        ],
        out_shape=[
            jax.ShapeDtypeStruct((sources, 2 * LANES, LANES), bf16),
            jax.ShapeDtypeStruct((n, LANES), bf16),
        ],
        input_output_aliases={} if half == 0 else {3: 0},
        compiler_params=params(60, dimension_semantics=("arbitrary",)),
        cost_estimate=pl.CostEstimate(
            flops=20_000_000_000, bytes_accessed=2 << 20, transcendentals=0
        ),
        name="attend",
    )(kv, r, *before)


def spread_kernel(in_ref, out_ref):
    for i in range(16):
        out_ref[i] = in_ref[...]


def spread(x):
    return pl.pallas_call(
        spread_kernel,
        out_shape=jax.ShapeDtypeStruct((16,) + x.shape, bf16),
        compiler_params=params(),
        cost_estimate=pl.CostEstimate(flops=0, bytes_accessed=1 << 20, transcendentals=0),
        name="spread",
    )(x)


def weight_kernel(me_ref, p0_ref, p1_ref, p2_ref, p3_ref, mem_ref, out_ref, total_ref, moved_ref):
    step = pl.program_id(0)
    sec = me_ref[0] // 2
    core = lax.rem(me_ref[0], 2)

    @pl.when(step == 0)
    def _():
        total = p0_ref[...].astype(f32) + p1_ref[...].astype(f32)
        total = total + (p2_ref[...].astype(f32) + p3_ref[...].astype(f32))
        total_ref[...] = total.astype(bf16)
        for i in range(16):
            for j in range(4):
                at = (sec ^ (j // 2)) * 512 + i * 32 + (core ^ (j % 2)) * 16
                rows = slice(i * 64 + j * 16, i * 64 + j * 16 + 16)
                moved_ref[rows, :] = total_ref[pl.ds(pl.multiple_of(at, 16), 16), :]

    grad = dot(mem_ref[...], moved_ref[...], TN).astype(bf16)
    for i in range(16):
        at = sec * 512 + step * 256 + (i // 2) * 32 + core * 16
        out_ref[i, 0:16, :] = grad[i * 16 : i * 16 + 16]
        out_ref[i, 16:32, :] = total_ref[pl.ds(pl.multiple_of(at, 16), 16), :]


def weight_blocks(me, parts, mem):
    n = mem.shape[0]
    part_spec = pl.BlockSpec((n, LANES), lambda s, me: (0, 0))
    return pl.pallas_call(
        weight_kernel,
        grid_spec=pltpu.PrefetchScalarGridSpec(
            num_scalar_prefetch=1,
            grid=(2,),
            in_specs=[part_spec] * 4 + [pl.BlockSpec((n, 256), lambda s, me: (0, s))],
            out_specs=pl.BlockSpec((16, 32, LANES), lambda s, me: (s, 0, 0)),
            scratch_shapes=[pltpu.VMEM((n, LANES), bf16), pltpu.VMEM((n, LANES), bf16)],
        ),
        out_shape=jax.ShapeDtypeStruct((32, 32, LANES), bf16),
        compiler_params=params(dimension_semantics=("arbitrary",)),
        cost_estimate=pl.CostEstimate(flops=0, bytes_accessed=6 << 20, transcendentals=0),
        name="weight_blocks",
    )(me, *parts, mem)


def finish_kernel(dp_ref, in_ref, wk_ref, wv_ref, mg_ref, wkg_ref, wvg_ref, acc_ref):
    p = pl.program_id(0)
    grads = []
    for i in range(4):
        cols = slice(i * LANES, (i + 1) * LANES)
        rows = [in_ref[4 * i + j, 0:16, :].astype(f32) for j in range(4)]
        wkg_ref[:, cols], wvg_ref[:, cols] = swap_halves(rows[0] + rows[1], rows[2] + rows[3])
        even = in_ref[pl.ds(4 * i + dp_ref[0], 1), 16:32, :][0].astype(f32)
        odd = in_ref[pl.ds(4 * i + 2 + dp_ref[0], 1), 16:32, :][0].astype(f32)
        grads.append(swap_halves(even, odd))
    kg = jnp.concatenate([x[0] for x in grads], 1).astype(bf16)
    vg = jnp.concatenate([x[1] for x in grads], 1).astype(bf16)
    part = dot(kg, wk_ref[...], NT) + dot(vg, wv_ref[...], NT)

    @pl.when(p == 0)
    def _():
        acc_ref[...] = part

    @pl.when(p > 0)
    def _():
        acc_ref[...] += part

    @pl.when(p == pl.num_programs(0) - 1)
    def _():
        mg_ref[0] = acc_ref[...].astype(bf16)


def finish(dp, x, wk, wv):
    d = wk.shape[0]
    w_spec = pl.BlockSpec((d, 512), lambda p, dp: (0, p))
    out_spec = pl.BlockSpec((16, 512), lambda p, dp: (0, p))
    shape = jax.ShapeDtypeStruct((16, wk.shape[1]), f32)
    return pl.pallas_call(
        finish_kernel,
        grid_spec=pltpu.PrefetchScalarGridSpec(
            num_scalar_prefetch=1,
            grid=(2,),
            in_specs=[pl.BlockSpec((16, 32, LANES), lambda p, dp: (p, 0, 0)), w_spec, w_spec],
            out_specs=[pl.BlockSpec((1, 16, d), lambda p, dp: (0, 0, 0)), out_spec, out_spec],
            scratch_shapes=[pltpu.VMEM((16, d), f32)],
        ),
        out_shape=[jax.ShapeDtypeStruct((1, 16, d), bf16), shape, shape],
        compiler_params=params(60, dimension_semantics=("arbitrary",)),
        cost_estimate=pl.CostEstimate(flops=0, bytes_accessed=12 << 20, transcendentals=0),
        name="finish",
    )(dp, x, wk, wv)


def exchange(x, axes):
    return lax.all_to_all(x, axes, 0, 0, tiled=True)


def crossed(x, k):
    return lax.ppermute(x, SUM_AXES, [(i, i ^ k) for i in range(4)])


def body(q, g, mem, wk, wv, target_modality, memory_modality, allow_pairs):
    me = lax.axis_index(SUM_AXES).reshape(1)
    dp = lax.axis_index("dp").reshape(1)
    mems = [mem] + [crossed(mem, k) for k in (1, 2, 3)]

    labels = jnp.arange(allow_pairs.shape[0], dtype=jnp.int32)
    q_onehot = (target_modality[0][:, None] == labels[None, :]).astype(f32)
    k_onehot = (memory_modality[0][:, None] == labels[None, :]).astype(f32)
    allowed = jnp.dot(jnp.dot(q_onehot, allow_pairs.astype(f32)), k_onehot.T) > 0.5
    allowed = allowed | (jnp.arange(allowed.shape[1], dtype=jnp.int32) == 0)[None, :]
    hide = jnp.where(allowed, 0.0, 1e30).astype(bf16).reshape(16, 2, 1)
    hide = jnp.broadcast_to(hide, (16, 2, HD)).reshape(16, LANES)

    first, second = prepare(me, q, g, hide, mems, wk, wv)
    first, mems = lax.optimization_barrier((first, mems))
    columns = jnp.concatenate(mems, 0).reshape(64, 2, 16, 2, 32)
    columns = lax.dynamic_index_in_dim(columns, me[0] // 2, 1, keepdims=False)
    columns = lax.dynamic_index_in_dim(columns, me[0] % 2, 2, keepdims=False)
    columns = spread(columns.reshape(64, 512))
    first = exchange(first, HEAD_AXES)
    first, second = lax.optimization_barrier((first, second))
    second = exchange(second, HEAD_AXES)
    columns, second = lax.optimization_barrier((columns, second))
    memory = exchange(columns, HEAD_AXES).reshape(1024, 512)

    q_grad, part = attend(0, first, first)
    q_grad, part = attend(1, first, second, part, q_grad)
    part, memory = lax.optimization_barrier((part, memory))
    q_grad = exchange(q_grad, HEAD_AXES)
    parts = [part] + [crossed(part, k) for k in (3, 2, 1)]
    blocks = weight_blocks(me, parts, memory)
    blocks, q_grad = lax.optimization_barrier((blocks, q_grad))
    blocks = exchange(blocks, HEAD_AXES + ("dp",))
    m_grad, wk_grad, wv_grad = finish(dp, blocks, wk, wv)
    return unpack_targets(q_grad), m_grad, wk_grad, wv_grad


def solution(mesh):
    fine = Mesh(mesh.devices.reshape(2, 4, 4, 2, 2), ALL_AXES)
    rows = P("dp", SAMPLE_AXES, None)
    in_specs = (rows, rows, rows, P(), P(), P("dp", SAMPLE_AXES), P("dp", None), P())
    out_specs = (rows, rows, P(ALL_AXES, None), P(ALL_AXES, None))
    return jax.shard_map(body, mesh=fine, in_specs=in_specs, out_specs=out_specs, check_vma=False)
```

```python
import functools

import jax
import jax.numpy as jnp
from jax import lax
from jax.experimental import pallas as pl
from jax.experimental.pallas import tpu as pltpu
from jax.sharding import Mesh, PartitionSpec as P

HD = 64
BLOCK = 128
LANES = 128
SCALE = 0.125
CHUNK = 256
NT = (((1,), (1,)), ((), ()))
NN = (((1,), (0,)), ((), ()))
TN = (((0,), (0,)), ((), ()))
HEAD_AXES = ("z", "y")
SUM_AXES = ("sec", "core")
SAMPLE_AXES = ("sec", "z", "y", "core")
ALL_AXES = ("sec", "z", "y", "core", "dp")
bf16 = jnp.bfloat16
f32 = jnp.float32


def dot(a, b, dims):
    return lax.dot_general(a, b, dims, preferred_element_type=f32)


def low_half():
    return lax.broadcasted_iota(jnp.int32, (1, LANES), 1) < HD


def swap_halves(a, b):
    lo = low_half()
    return jnp.where(lo, a, pltpu.roll(b, HD, 1)), jnp.where(lo, pltpu.roll(a, HD, 1), b)


def params(mib=48, **kw):
    return pltpu.CompilerParams(vmem_limit_bytes=mib << 20, **kw)


ROWS = (336, 272)
KV_ROW = 256
STEP = 4


def prepare_kernel(me_ref, q_ref, g_ref, hide_ref, m0_ref, m1_ref, m2_ref, m3_ref, wk_ref, wv_ref, *out_refs):
    mem = jnp.concatenate([m0_ref[0], m1_ref[0], m2_ref[0], m3_ref[0]], 0)
    keys = dot(mem, wk_ref[...], NN)
    values = dot(mem, wv_ref[...], NN)
    for i in range(2):
        cols = slice(i * LANES, (i + 1) * LANES)
        for t, out_ref in enumerate(out_refs):
            for k, ref in enumerate((q_ref, g_ref)):
                a = ref[0, t * 256 : t * 256 + 128, cols].astype(f32)
                b = ref[0, t * 256 + 128 : t * 256 + 256, cols].astype(f32)
                even, odd = swap_halves(a, b)
                out_ref[2 * i, k * 128 : k * 128 + 128, :] = even.astype(bf16)
                out_ref[2 * i + 1, k * 128 : k * 128 + 128, :] = odd.astype(bf16)
            for n in range(2):
                out_ref[2 * i + n, ROWS[t] - 16 : ROWS[t], :] = hide_ref[...]
        for n, x in enumerate(swap_halves(keys[:, cols], values[:, cols])):
            x = x.astype(bf16)
            for j in range(4):
                at = pl.multiple_of(KV_ROW + (me_ref[0] ^ j) * 16, 16)
                out_refs[0][2 * i + n, pl.ds(at, 16), :] = x[j * 16 : j * 16 + 16]


def prepare(me, q, g, hide, mems, wk, wv):
    d = wk.shape[0]
    target_spec = pl.BlockSpec((1, 512, 256), lambda p, me: (0, 0, p))
    mem_spec = pl.BlockSpec((1, 16, d), lambda p, me: (0, 0, 0))
    w_spec = pl.BlockSpec((d, 256), lambda p, me: (0, p))
    return pl.pallas_call(
        prepare_kernel,
        grid_spec=pltpu.PrefetchScalarGridSpec(
            num_scalar_prefetch=1,
            grid=(4,),
            in_specs=[target_spec] * 2
            + [pl.BlockSpec((16, LANES), lambda p, me: (0, 0))]
            + [mem_spec] * 4
            + [w_spec] * 2,
            out_specs=[pl.BlockSpec((4, rows, LANES), lambda p, me: (p, 0, 0)) for rows in ROWS],
        ),
        out_shape=[jax.ShapeDtypeStruct((16, rows, LANES), bf16) for rows in ROWS],
        compiler_params=params(60),
        cost_estimate=pl.CostEstimate(flops=0, bytes_accessed=16 << 20, transcendentals=0),
        name="prepare",
    )(me, q, g, hide, *mems, wk, wv)


def unpack_kernel(in_ref, out_ref):
    for i in range(2):
        for t in range(2):
            even = in_ref[2 * i, t * 128 : t * 128 + 128, :].astype(f32)
            odd = in_ref[2 * i + 1, t * 128 : t * 128 + 128, :].astype(f32)
            a, b = swap_halves(even, odd)
            cols = slice(i * LANES, (i + 1) * LANES)
            out_ref[0, t * 256 : t * 256 + 128, cols] = a.astype(bf16)
            out_ref[0, t * 256 + 128 : t * 256 + 256, cols] = b.astype(bf16)


def unpack_targets(x):
    return pl.pallas_call(
        unpack_kernel,
        grid=(4,),
        in_specs=[pl.BlockSpec((4, 256, LANES), lambda p: (p, 0, 0))],
        out_specs=pl.BlockSpec((1, 512, 256), lambda p: (0, 0, p)),
        out_shape=jax.ShapeDtypeStruct((1, 512, 1024), bf16),
        compiler_params=params(),
        cost_estimate=pl.CostEstimate(flops=0, bytes_accessed=6 << 20, transcendentals=0),
        name="unpack_targets",
    )(x)


def one_tile(q, g, away, k2_ref, v2_ref, kt_ref, ka_ref, va_ref):
    lo = low_half()
    n = k2_ref.shape[0]
    per = CHUNK // BLOCK
    chunks = n // CHUNK
    rows = [slice(c * CHUNK, c * CHUNK + CHUNK) for c in range(chunks)]
    q = q * jnp.asarray(SCALE, bf16)
    zero = jnp.zeros_like(q)
    q2 = jnp.concatenate([jnp.where(lo, q, zero), jnp.where(lo, zero, q)], 0)
    g2 = jnp.concatenate([jnp.where(lo, g, zero), jnp.where(lo, zero, g)], 0)
    scores = [dot(k2_ref[r, :], q2, NT) for r in rows]
    other = pltpu.roll(away, HD, 1)
    away = (jnp.where(lo, away, other), jnp.where(lo, other, away))
    hidden = []
    top = None
    for j in range(n // BLOCK):
        part = scores[j // per][(j % per) * BLOCK : (j % per + 1) * BLOCK]
        at = j // 2
        hide = jnp.concatenate([away[j % 2][at : at + 1], away[j % 2][4 + at : 5 + at]], 1)
        hidden.append(hide)
        part_top = jnp.max(part, axis=0, keepdims=True) - hide
        top = part_top if top is None else jnp.maximum(top, part_top)
    expd = []
    total = None
    for c in range(chunks):
        parts = [
            jnp.exp(scores[c][i * BLOCK : (i + 1) * BLOCK] - (top + hidden[c * per + i]))
            for i in range(per)
        ]
        e = jnp.concatenate(parts, 0)
        expd.append(e)
        s = jnp.sum(e, axis=0, keepdims=True)
        total = s if total is None else total + s
    inverse = 1.0 / total
    dprobs = []
    delta = None
    for c in range(chunks):
        dp = dot(v2_ref[rows[c], :], g2, NT)
        dprobs.append(dp)
        s = jnp.sum(expd[c] * dp, axis=0, keepdims=True)
        delta = s if delta is None else delta + s
    delta = delta * inverse
    qgt = None
    for c in range(chunks):
        p = expd[c] * inverse
        ds = (p * (dprobs[c] - delta)).astype(bf16)
        va_ref[rows[c], :] += dot(p.astype(bf16), g2, NN)
        ka_ref[rows[c], :] += dot(ds, q2, NN)
        x = dot(kt_ref[:, rows[c]], ds, NN)
        qgt = x if qgt is None else qgt + x
    qgt = qgt * SCALE
    both = jnp.concatenate([qgt[:, :LANES], qgt[:, LANES:]], 0)
    return jnp.transpose(both).astype(bf16)


def attend_kernel(*refs, half):
    if half == 0:
        kv_ref, r_ref, qg_ref, kvg_ref, k2_ref, v2_ref, kt_ref, ka_ref, va_ref = refs
    else:
        kv_ref, r_ref, before_ref, _, qg_ref, kvg_ref, k2_ref, v2_ref, kt_ref, ka_ref, va_ref = refs
    lo = low_half()

    @pl.when(pl.program_id(0) == 0)
    def _():
        order = [(i, j * 32) for j in range(2) for i in range(16)]
        kv = jnp.concatenate([kv_ref[i, at : at + 32, :] for i, at in order], 0).astype(f32)
        swapped = pltpu.roll(kv, HD, 1)
        k2 = jnp.where(lo, kv, swapped)
        k2_ref[...] = k2.astype(bf16)
        v2_ref[...] = jnp.where(lo, swapped, kv).astype(bf16)
        kt_ref[...] = jnp.transpose(k2)[:HD].astype(bf16)
        ka_ref[...] = jnp.zeros_like(ka_ref)
        va_ref[...] = jnp.zeros_like(va_ref)

    for i in range(STEP):
        away = r_ref[i, ROWS[half] - 16 : ROWS[half], :].astype(f32)[half * 8 : half * 8 + 8]
        q = r_ref[i, 0:128, :]
        g = r_ref[i, 128:256, :]
        qg_ref[i] = one_tile(q, g, away, k2_ref, v2_ref, kt_ref, ka_ref, va_ref)

    @pl.when(pl.program_id(0) == pl.num_programs(0) - 1)
    def _():
        ka = ka_ref[...]
        va = va_ref[...]
        ka = ka + pltpu.roll(ka, HD, 1)
        va = va + pltpu.roll(va, HD, 1)
        kvg = jnp.where(lo, ka, va)
        if half == 1:
            kvg = kvg + before_ref[...].astype(f32)
        kvg_ref[...] = kvg.astype(bf16)


def attend(half, kv, r, *before):
    sources = r.shape[0]
    n = 64 * sources
    whole = pl.BlockSpec((n, LANES), lambda i: (0, 0))
    return pl.pallas_call(
        functools.partial(attend_kernel, half=half),
        grid=(sources // STEP,),
        in_specs=[
            pl.BlockSpec((sources, 64, LANES), lambda i: (0, KV_ROW // 64, 0)),
            pl.BlockSpec((STEP, ROWS[half], LANES), lambda i: (i, 0, 0)),
        ]
        + ([] if half == 0 else [whole, pl.BlockSpec(memory_space=pl.ANY)]),
        out_specs=[pl.BlockSpec((STEP, LANES, LANES), lambda i: (i, half, 0)), whole],
        scratch_shapes=[
            pltpu.VMEM((n, LANES), bf16),
            pltpu.VMEM((n, LANES), bf16),
            pltpu.VMEM((HD, n), bf16),
            pltpu.VMEM((n, LANES), f32),
            pltpu.VMEM((n, LANES), f32),
        ],
        out_shape=[
            jax.ShapeDtypeStruct((sources, 2 * LANES, LANES), bf16),
            jax.ShapeDtypeStruct((n, LANES), bf16),
        ],
        input_output_aliases={} if half == 0 else {3: 0},
        compiler_params=params(60, dimension_semantics=("arbitrary",)),
        cost_estimate=pl.CostEstimate(
            flops=20_000_000_000, bytes_accessed=2 << 20, transcendentals=0
        ),
        name="attend",
    )(kv, r, *before)


def spread_kernel(in_ref, out_ref):
    for i in range(16):
        out_ref[i] = in_ref[...]


def spread(x):
    return pl.pallas_call(
        spread_kernel,
        out_shape=jax.ShapeDtypeStruct((16,) + x.shape, bf16),
        compiler_params=params(),
        cost_estimate=pl.CostEstimate(flops=0, bytes_accessed=1 << 20, transcendentals=0),
        name="spread",
    )(x)


def weight_kernel(me_ref, p0_ref, p1_ref, mem_ref, out_ref, total_ref, moved_ref):
    step = pl.program_id(0)
    sec = me_ref[0] // 2
    core = lax.rem(me_ref[0], 2)

    @pl.when(step == 0)
    def _():
        total = p0_ref[...].astype(f32) + p1_ref[...].astype(f32)
        total_ref[...] = total.astype(bf16)
        for i in range(16):
            for j in range(4):
                at = (sec ^ (j // 2)) * 512 + i * 32 + (core ^ (j % 2)) * 16
                rows = slice(i * 64 + j * 16, i * 64 + j * 16 + 16)
                moved_ref[rows, :] = total_ref[pl.ds(pl.multiple_of(at, 16), 16), :]

    grad = dot(mem_ref[...], moved_ref[...], TN).astype(bf16)
    for i in range(16):
        at = sec * 512 + step * 256 + (i // 2) * 32 + core * 16
        out_ref[i, 0:16, :] = grad[i * 16 : i * 16 + 16]
        out_ref[i, 16:32, :] = total_ref[pl.ds(pl.multiple_of(at, 16), 16), :]


def weight_blocks(me, parts, mem):
    n = mem.shape[0]
    part_spec = pl.BlockSpec((n, LANES), lambda s, me: (0, 0))
    return pl.pallas_call(
        weight_kernel,
        grid_spec=pltpu.PrefetchScalarGridSpec(
            num_scalar_prefetch=1,
            grid=(2,),
            in_specs=[part_spec] * 2 + [pl.BlockSpec((n, 256), lambda s, me: (0, s))],
            out_specs=pl.BlockSpec((16, 32, LANES), lambda s, me: (s, 0, 0)),
            scratch_shapes=[pltpu.VMEM((n, LANES), bf16), pltpu.VMEM((n, LANES), bf16)],
        ),
        out_shape=jax.ShapeDtypeStruct((32, 32, LANES), bf16),
        compiler_params=params(dimension_semantics=("arbitrary",)),
        cost_estimate=pl.CostEstimate(flops=0, bytes_accessed=6 << 20, transcendentals=0),
        name="weight_blocks",
    )(me, *parts, mem)


def finish_kernel(dp_ref, in_ref, wk_ref, wv_ref, mg_ref, wkg_ref, wvg_ref, acc_ref):
    p = pl.program_id(0)
    grads = []
    for i in range(4):
        cols = slice(i * LANES, (i + 1) * LANES)
        rows = [in_ref[4 * i + j, 0:16, :].astype(f32) for j in range(4)]
        wkg_ref[:, cols], wvg_ref[:, cols] = swap_halves(rows[0] + rows[1], rows[2] + rows[3])
        even = in_ref[pl.ds(4 * i + dp_ref[0], 1), 16:32, :][0].astype(f32)
        odd = in_ref[pl.ds(4 * i + 2 + dp_ref[0], 1), 16:32, :][0].astype(f32)
        grads.append(swap_halves(even, odd))
    kg = jnp.concatenate([x[0] for x in grads], 1).astype(bf16)
    vg = jnp.concatenate([x[1] for x in grads], 1).astype(bf16)
    part = dot(kg, wk_ref[...], NT) + dot(vg, wv_ref[...], NT)

    @pl.when(p == 0)
    def _():
        acc_ref[...] = part

    @pl.when(p > 0)
    def _():
        acc_ref[...] += part

    @pl.when(p == pl.num_programs(0) - 1)
    def _():
        mg_ref[0] = acc_ref[...].astype(bf16)


def finish(dp, x, wk, wv):
    d = wk.shape[0]
    w_spec = pl.BlockSpec((d, 512), lambda p, dp: (0, p))
    out_spec = pl.BlockSpec((16, 512), lambda p, dp: (0, p))
    shape = jax.ShapeDtypeStruct((16, wk.shape[1]), f32)
    return pl.pallas_call(
        finish_kernel,
        grid_spec=pltpu.PrefetchScalarGridSpec(
            num_scalar_prefetch=1,
            grid=(2,),
            in_specs=[pl.BlockSpec((16, 32, LANES), lambda p, dp: (p, 0, 0)), w_spec, w_spec],
            out_specs=[pl.BlockSpec((1, 16, d), lambda p, dp: (0, 0, 0)), out_spec, out_spec],
            scratch_shapes=[pltpu.VMEM((16, d), f32)],
        ),
        out_shape=[jax.ShapeDtypeStruct((1, 16, d), bf16), shape, shape],
        compiler_params=params(60, dimension_semantics=("arbitrary",)),
        cost_estimate=pl.CostEstimate(flops=0, bytes_accessed=12 << 20, transcendentals=0),
        name="finish",
    )(dp, x, wk, wv)


def exchange(x, axes):
    return lax.all_to_all(x, axes, 0, 0, tiled=True)


def crossed(x, k):
    return lax.ppermute(x, SUM_AXES, [(i, i ^ k) for i in range(4)])


def body(q, g, mem, wk, wv, target_modality, memory_modality, allow_pairs):
    me = lax.axis_index(SUM_AXES).reshape(1)
    dp = lax.axis_index("dp").reshape(1)
    mems = [mem] + [crossed(mem, k) for k in (1, 2, 3)]

    labels = jnp.arange(allow_pairs.shape[0], dtype=jnp.int32)
    q_onehot = (target_modality[0][:, None] == labels[None, :]).astype(f32)
    k_onehot = (memory_modality[0][:, None] == labels[None, :]).astype(f32)
    allowed = jnp.dot(jnp.dot(q_onehot, allow_pairs.astype(f32)), k_onehot.T) > 0.5
    allowed = allowed | (jnp.arange(allowed.shape[1], dtype=jnp.int32) == 0)[None, :]
    hide = jnp.where(allowed, 0.0, 1e30).astype(bf16).reshape(16, 2, 1)
    hide = jnp.broadcast_to(hide, (16, 2, HD)).reshape(16, LANES)

    first, second = prepare(me, q, g, hide, mems, wk, wv)
    first, mems = lax.optimization_barrier((first, mems))
    columns = jnp.concatenate(mems, 0).reshape(64, 2, 16, 2, 32)
    columns = lax.dynamic_index_in_dim(columns, me[0] // 2, 1, keepdims=False)
    columns = lax.dynamic_index_in_dim(columns, me[0] % 2, 2, keepdims=False)
    columns = spread(columns.reshape(64, 512))
    first = exchange(first, HEAD_AXES)
    first, second = lax.optimization_barrier((first, second))
    second = exchange(second, HEAD_AXES)
    columns, second = lax.optimization_barrier((columns, second))
    memory = exchange(columns, HEAD_AXES).reshape(1024, 512)

    q_grad, part = attend(0, first, first)
    q_grad, part = attend(1, first, second, part, q_grad)
    part, memory = lax.optimization_barrier((part, memory))
    q_grad = exchange(q_grad, HEAD_AXES)
    pair = (part.astype(f32) + crossed(part, 1).astype(f32)).astype(bf16)
    blocks = weight_blocks(me, [pair, crossed(pair, 2)], memory)
    blocks, q_grad = lax.optimization_barrier((blocks, q_grad))
    blocks = exchange(blocks, HEAD_AXES + ("dp",))
    m_grad, wk_grad, wv_grad = finish(dp, blocks, wk, wv)
    return unpack_targets(q_grad), m_grad, wk_grad, wv_grad


def solution(mesh):
    fine = Mesh(mesh.devices.reshape(2, 4, 4, 2, 2), ALL_AXES)
    rows = P("dp", SAMPLE_AXES, None)
    in_specs = (rows, rows, rows, P(), P(), P("dp", SAMPLE_AXES), P("dp", None), P())
    out_specs = (rows, rows, P(ALL_AXES, None), P(ALL_AXES, None))
    return jax.shard_map(body, mesh=fine, in_specs=in_specs, out_specs=out_specs, check_vma=False)
```

```python
import functools

import jax
import jax.numpy as jnp
from jax import lax
from jax.experimental import pallas as pl
from jax.experimental.pallas import tpu as pltpu
from jax.sharding import Mesh, PartitionSpec as P

HD = 64
BLOCK = 128
LANES = 128
SCALE = 0.125
CHUNK = 256
NT = (((1,), (1,)), ((), ()))
NN = (((1,), (0,)), ((), ()))
TN = (((0,), (0,)), ((), ()))
HEAD_AXES = ("z", "y")
SUM_AXES = ("sec", "core")
SAMPLE_AXES = ("sec", "z", "y", "core")
ALL_AXES = ("sec", "z", "y", "core", "dp")
bf16 = jnp.bfloat16
f32 = jnp.float32


def dot(a, b, dims):
    return lax.dot_general(a, b, dims, preferred_element_type=f32)


def low_half():
    return lax.broadcasted_iota(jnp.int32, (1, LANES), 1) < HD


def swap_halves(a, b):
    lo = low_half()
    return jnp.where(lo, a, pltpu.roll(b, HD, 1)), jnp.where(lo, pltpu.roll(a, HD, 1), b)


def params(mib=48, **kw):
    return pltpu.CompilerParams(vmem_limit_bytes=mib << 20, **kw)


ROWS = (336, 272)
KV_ROW = 256
STEP = 4


def prepare_kernel(me_ref, q_ref, g_ref, hide_ref, m0_ref, m1_ref, m2_ref, m3_ref, wk_ref, wv_ref, *out_refs):
    mem = jnp.concatenate([m0_ref[0], m1_ref[0], m2_ref[0], m3_ref[0]], 0)
    keys = dot(mem, wk_ref[...], NN)
    values = dot(mem, wv_ref[...], NN)
    for i in range(4):
        cols = slice(i * LANES, (i + 1) * LANES)
        for t, out_ref in enumerate(out_refs):
            for k, ref in enumerate((q_ref, g_ref)):
                a = ref[0, t * 256 : t * 256 + 128, cols].astype(f32)
                b = ref[0, t * 256 + 128 : t * 256 + 256, cols].astype(f32)
                even, odd = swap_halves(a, b)
                out_ref[2 * i, k * 128 : k * 128 + 128, :] = even.astype(bf16)
                out_ref[2 * i + 1, k * 128 : k * 128 + 128, :] = odd.astype(bf16)
            for n in range(2):
                out_ref[2 * i + n, ROWS[t] - 16 : ROWS[t], :] = hide_ref[...]
        for n, x in enumerate(swap_halves(keys[:, cols], values[:, cols])):
            x = x.astype(bf16)
            for j in range(4):
                at = pl.multiple_of(KV_ROW + (me_ref[0] ^ j) * 16, 16)
                out_refs[0][2 * i + n, pl.ds(at, 16), :] = x[j * 16 : j * 16 + 16]


def prepare(me, q, g, hide, mems, wk, wv):
    d = wk.shape[0]
    target_spec = pl.BlockSpec((1, 512, 512), lambda p, me: (0, 0, p))
    mem_spec = pl.BlockSpec((1, 16, d), lambda p, me: (0, 0, 0))
    w_spec = pl.BlockSpec((d, 512), lambda p, me: (0, p))
    return pl.pallas_call(
        prepare_kernel,
        grid_spec=pltpu.PrefetchScalarGridSpec(
            num_scalar_prefetch=1,
            grid=(2,),
            in_specs=[target_spec] * 2
            + [pl.BlockSpec((16, LANES), lambda p, me: (0, 0))]
            + [mem_spec] * 4
            + [w_spec] * 2,
            out_specs=[pl.BlockSpec((8, rows, LANES), lambda p, me: (p, 0, 0)) for rows in ROWS],
        ),
        out_shape=[jax.ShapeDtypeStruct((16, rows, LANES), bf16) for rows in ROWS],
        compiler_params=params(60),
        cost_estimate=pl.CostEstimate(flops=0, bytes_accessed=16 << 20, transcendentals=0),
        name="prepare",
    )(me, q, g, hide, *mems, wk, wv)


def unpack_kernel(in_ref, out_ref):
    for i in range(2):
        for t in range(2):
            even = in_ref[2 * i, t * 128 : t * 128 + 128, :].astype(f32)
            odd = in_ref[2 * i + 1, t * 128 : t * 128 + 128, :].astype(f32)
            a, b = swap_halves(even, odd)
            cols = slice(i * LANES, (i + 1) * LANES)
            out_ref[0, t * 256 : t * 256 + 128, cols] = a.astype(bf16)
            out_ref[0, t * 256 + 128 : t * 256 + 256, cols] = b.astype(bf16)


def unpack_targets(x):
    return pl.pallas_call(
        unpack_kernel,
        grid=(4,),
        in_specs=[pl.BlockSpec((4, 256, LANES), lambda p: (p, 0, 0))],
        out_specs=pl.BlockSpec((1, 512, 256), lambda p: (0, 0, p)),
        out_shape=jax.ShapeDtypeStruct((1, 512, 1024), bf16),
        compiler_params=params(),
        cost_estimate=pl.CostEstimate(flops=0, bytes_accessed=6 << 20, transcendentals=0),
        name="unpack_targets",
    )(x)


def one_tile(q, g, away, k2_ref, v2_ref, kt_ref, ka_ref, va_ref):
    lo = low_half()
    n = k2_ref.shape[0]
    per = CHUNK // BLOCK
    chunks = n // CHUNK
    rows = [slice(c * CHUNK, c * CHUNK + CHUNK) for c in range(chunks)]
    q = q * jnp.asarray(SCALE, bf16)
    zero = jnp.zeros_like(q)
    q2 = jnp.concatenate([jnp.where(lo, q, zero), jnp.where(lo, zero, q)], 0)
    g2 = jnp.concatenate([jnp.where(lo, g, zero), jnp.where(lo, zero, g)], 0)
    scores = [dot(k2_ref[r, :], q2, NT) for r in rows]
    other = pltpu.roll(away, HD, 1)
    away = (jnp.where(lo, away, other), jnp.where(lo, other, away))
    hidden = []
    top = None
    for j in range(n // BLOCK):
        part = scores[j // per][(j % per) * BLOCK : (j % per + 1) * BLOCK]
        at = j // 2
        hide = jnp.concatenate([away[j % 2][at : at + 1], away[j % 2][4 + at : 5 + at]], 1)
        hidden.append(hide)
        part_top = jnp.max(part, axis=0, keepdims=True) - hide
        top = part_top if top is None else jnp.maximum(top, part_top)
    expd = []
    total = None
    for c in range(chunks):
        parts = [
            jnp.exp(scores[c][i * BLOCK : (i + 1) * BLOCK] - (top + hidden[c * per + i]))
            for i in range(per)
        ]
        e = jnp.concatenate(parts, 0)
        expd.append(e)
        s = jnp.sum(e, axis=0, keepdims=True)
        total = s if total is None else total + s
    inverse = 1.0 / total
    dprobs = []
    delta = None
    for c in range(chunks):
        dp = dot(v2_ref[rows[c], :], g2, NT)
        dprobs.append(dp)
        s = jnp.sum(expd[c] * dp, axis=0, keepdims=True)
        delta = s if delta is None else delta + s
    delta = delta * inverse
    qgt = None
    for c in range(chunks):
        p = expd[c] * inverse
        ds = (p * (dprobs[c] - delta)).astype(bf16)
        va_ref[rows[c], :] += dot(p.astype(bf16), g2, NN)
        ka_ref[rows[c], :] += dot(ds, q2, NN)
        x = dot(kt_ref[:, rows[c]], ds, NN)
        qgt = x if qgt is None else qgt + x
    qgt = qgt * SCALE
    both = jnp.concatenate([qgt[:, :LANES], qgt[:, LANES:]], 0)
    return jnp.transpose(both).astype(bf16)


def attend_kernel(*refs, half):
    if half == 0:
        kv_ref, r_ref, qg_ref, kvg_ref, k2_ref, v2_ref, kt_ref, ka_ref, va_ref = refs
    else:
        kv_ref, r_ref, before_ref, _, qg_ref, kvg_ref, k2_ref, v2_ref, kt_ref, ka_ref, va_ref = refs
    lo = low_half()

    @pl.when(pl.program_id(0) == 0)
    def _():
        order = [(i, j * 32) for j in range(2) for i in range(16)]
        kv = jnp.concatenate([kv_ref[i, at : at + 32, :] for i, at in order], 0).astype(f32)
        swapped = pltpu.roll(kv, HD, 1)
        k2 = jnp.where(lo, kv, swapped)
        k2_ref[...] = k2.astype(bf16)
        v2_ref[...] = jnp.where(lo, swapped, kv).astype(bf16)
        kt_ref[...] = jnp.transpose(k2)[:HD].astype(bf16)
        ka_ref[...] = jnp.zeros_like(ka_ref)
        va_ref[...] = jnp.zeros_like(va_ref)

    for i in range(STEP):
        away = r_ref[i, ROWS[half] - 16 : ROWS[half], :].astype(f32)[half * 8 : half * 8 + 8]
        q = r_ref[i, 0:128, :]
        g = r_ref[i, 128:256, :]
        qg_ref[i] = one_tile(q, g, away, k2_ref, v2_ref, kt_ref, ka_ref, va_ref)

    @pl.when(pl.program_id(0) == pl.num_programs(0) - 1)
    def _():
        ka = ka_ref[...]
        va = va_ref[...]
        ka = ka + pltpu.roll(ka, HD, 1)
        va = va + pltpu.roll(va, HD, 1)
        kvg = jnp.where(lo, ka, va)
        if half == 1:
            kvg = kvg + before_ref[...].astype(f32)
        kvg_ref[...] = kvg.astype(bf16)


def attend(half, kv, r, *before):
    sources = r.shape[0]
    n = 64 * sources
    whole = pl.BlockSpec((n, LANES), lambda i: (0, 0))
    return pl.pallas_call(
        functools.partial(attend_kernel, half=half),
        grid=(sources // STEP,),
        in_specs=[
            pl.BlockSpec((sources, 64, LANES), lambda i: (0, KV_ROW // 64, 0)),
            pl.BlockSpec((STEP, ROWS[half], LANES), lambda i: (i, 0, 0)),
        ]
        + ([] if half == 0 else [whole, pl.BlockSpec(memory_space=pl.ANY)]),
        out_specs=[pl.BlockSpec((STEP, LANES, LANES), lambda i: (i, half, 0)), whole],
        scratch_shapes=[
            pltpu.VMEM((n, LANES), bf16),
            pltpu.VMEM((n, LANES), bf16),
            pltpu.VMEM((HD, n), bf16),
            pltpu.VMEM((n, LANES), f32),
            pltpu.VMEM((n, LANES), f32),
        ],
        out_shape=[
            jax.ShapeDtypeStruct((sources, 2 * LANES, LANES), bf16),
            jax.ShapeDtypeStruct((n, LANES), bf16),
        ],
        input_output_aliases={} if half == 0 else {3: 0},
        compiler_params=params(60, dimension_semantics=("arbitrary",)),
        cost_estimate=pl.CostEstimate(
            flops=20_000_000_000, bytes_accessed=2 << 20, transcendentals=0
        ),
        name="attend",
    )(kv, r, *before)


def spread_kernel(in_ref, out_ref):
    for i in range(16):
        out_ref[i] = in_ref[...]


def spread(x):
    return pl.pallas_call(
        spread_kernel,
        out_shape=jax.ShapeDtypeStruct((16,) + x.shape, bf16),
        compiler_params=params(),
        cost_estimate=pl.CostEstimate(flops=0, bytes_accessed=1 << 20, transcendentals=0),
        name="spread",
    )(x)


def weight_kernel(me_ref, p0_ref, p1_ref, mem_ref, out_ref, total_ref, moved_ref):
    step = pl.program_id(0)
    sec = me_ref[0] // 2
    core = lax.rem(me_ref[0], 2)

    @pl.when(step == 0)
    def _():
        total = p0_ref[...].astype(f32) + p1_ref[...].astype(f32)
        total_ref[...] = total.astype(bf16)
        for i in range(16):
            for j in range(4):
                at = (sec ^ (j // 2)) * 512 + i * 32 + (core ^ (j % 2)) * 16
                rows = slice(i * 64 + j * 16, i * 64 + j * 16 + 16)
                moved_ref[rows, :] = total_ref[pl.ds(pl.multiple_of(at, 16), 16), :]

    grad = dot(mem_ref[...], moved_ref[...], TN).astype(bf16)
    for i in range(16):
        at = sec * 512 + step * 256 + (i // 2) * 32 + core * 16
        out_ref[i, 0:16, :] = grad[i * 16 : i * 16 + 16]
        out_ref[i, 16:32, :] = total_ref[pl.ds(pl.multiple_of(at, 16), 16), :]


def weight_blocks(me, parts, mem):
    n = mem.shape[0]
    part_spec = pl.BlockSpec((n, LANES), lambda s, me: (0, 0))
    return pl.pallas_call(
        weight_kernel,
        grid_spec=pltpu.PrefetchScalarGridSpec(
            num_scalar_prefetch=1,
            grid=(2,),
            in_specs=[part_spec] * 2 + [pl.BlockSpec((n, 256), lambda s, me: (0, s))],
            out_specs=pl.BlockSpec((16, 32, LANES), lambda s, me: (s, 0, 0)),
            scratch_shapes=[pltpu.VMEM((n, LANES), bf16), pltpu.VMEM((n, LANES), bf16)],
        ),
        out_shape=jax.ShapeDtypeStruct((32, 32, LANES), bf16),
        compiler_params=params(dimension_semantics=("arbitrary",)),
        cost_estimate=pl.CostEstimate(flops=0, bytes_accessed=6 << 20, transcendentals=0),
        name="weight_blocks",
    )(me, *parts, mem)


def finish_kernel(dp_ref, in_ref, wk_ref, wv_ref, mg_ref, wkg_ref, wvg_ref, acc_ref):
    p = pl.program_id(0)
    grads = []
    for i in range(4):
        cols = slice(i * LANES, (i + 1) * LANES)
        rows = [in_ref[4 * i + j, 0:16, :].astype(f32) for j in range(4)]
        wkg_ref[:, cols], wvg_ref[:, cols] = swap_halves(rows[0] + rows[1], rows[2] + rows[3])
        even = in_ref[pl.ds(4 * i + dp_ref[0], 1), 16:32, :][0].astype(f32)
        odd = in_ref[pl.ds(4 * i + 2 + dp_ref[0], 1), 16:32, :][0].astype(f32)
        grads.append(swap_halves(even, odd))
    kg = jnp.concatenate([x[0] for x in grads], 1).astype(bf16)
    vg = jnp.concatenate([x[1] for x in grads], 1).astype(bf16)
    part = dot(kg, wk_ref[...], NT) + dot(vg, wv_ref[...], NT)

    @pl.when(p == 0)
    def _():
        acc_ref[...] = part

    @pl.when(p > 0)
    def _():
        acc_ref[...] += part

    @pl.when(p == pl.num_programs(0) - 1)
    def _():
        mg_ref[0] = acc_ref[...].astype(bf16)


def finish(dp, x, wk, wv):
    d = wk.shape[0]
    w_spec = pl.BlockSpec((d, 512), lambda p, dp: (0, p))
    out_spec = pl.BlockSpec((16, 512), lambda p, dp: (0, p))
    shape = jax.ShapeDtypeStruct((16, wk.shape[1]), f32)
    return pl.pallas_call(
        finish_kernel,
        grid_spec=pltpu.PrefetchScalarGridSpec(
            num_scalar_prefetch=1,
            grid=(2,),
            in_specs=[pl.BlockSpec((16, 32, LANES), lambda p, dp: (p, 0, 0)), w_spec, w_spec],
            out_specs=[pl.BlockSpec((1, 16, d), lambda p, dp: (0, 0, 0)), out_spec, out_spec],
            scratch_shapes=[pltpu.VMEM((16, d), f32)],
        ),
        out_shape=[jax.ShapeDtypeStruct((1, 16, d), bf16), shape, shape],
        compiler_params=params(60, dimension_semantics=("arbitrary",)),
        cost_estimate=pl.CostEstimate(flops=0, bytes_accessed=12 << 20, transcendentals=0),
        name="finish",
    )(dp, x, wk, wv)


def exchange(x, axes):
    return lax.all_to_all(x, axes, 0, 0, tiled=True)


def crossed(x, k):
    return lax.ppermute(x, SUM_AXES, [(i, i ^ k) for i in range(4)])


def body(q, g, mem, wk, wv, target_modality, memory_modality, allow_pairs):
    me = lax.axis_index(SUM_AXES).reshape(1)
    dp = lax.axis_index("dp").reshape(1)
    mems = [mem] + [crossed(mem, k) for k in (1, 2, 3)]

    labels = jnp.arange(allow_pairs.shape[0], dtype=jnp.int32)
    q_onehot = (target_modality[0][:, None] == labels[None, :]).astype(f32)
    k_onehot = (memory_modality[0][:, None] == labels[None, :]).astype(f32)
    allowed = jnp.dot(jnp.dot(q_onehot, allow_pairs.astype(f32)), k_onehot.T) > 0.5
    allowed = allowed | (jnp.arange(allowed.shape[1], dtype=jnp.int32) == 0)[None, :]
    hide = jnp.where(allowed, 0.0, 1e30).astype(bf16).reshape(16, 2, 1)
    hide = jnp.broadcast_to(hide, (16, 2, HD)).reshape(16, LANES)

    first, second = prepare(me, q, g, hide, mems, wk, wv)
    first, mems = lax.optimization_barrier((first, mems))
    columns = jnp.concatenate(mems, 0).reshape(64, 2, 16, 2, 32)
    columns = lax.dynamic_index_in_dim(columns, me[0] // 2, 1, keepdims=False)
    columns = lax.dynamic_index_in_dim(columns, me[0] % 2, 2, keepdims=False)
    columns = spread(columns.reshape(64, 512))
    first = exchange(first, HEAD_AXES)
    first, second = lax.optimization_barrier((first, second))
    second = exchange(second, HEAD_AXES)
    columns, second = lax.optimization_barrier((columns, second))
    memory = exchange(columns, HEAD_AXES).reshape(1024, 512)

    q_grad, part = attend(0, first, first)
    q_grad, part = attend(1, first, second, part, q_grad)
    part, memory = lax.optimization_barrier((part, memory))
    q_grad = exchange(q_grad, HEAD_AXES)
    pair = (part.astype(f32) + crossed(part, 1).astype(f32)).astype(bf16)
    blocks = weight_blocks(me, [pair, crossed(pair, 2)], memory)
    blocks, q_grad = lax.optimization_barrier((blocks, q_grad))
    blocks = exchange(blocks, HEAD_AXES + ("dp",))
    m_grad, wk_grad, wv_grad = finish(dp, blocks, wk, wv)
    return unpack_targets(q_grad), m_grad, wk_grad, wv_grad


def solution(mesh):
    fine = Mesh(mesh.devices.reshape(2, 4, 4, 2, 2), ALL_AXES)
    rows = P("dp", SAMPLE_AXES, None)
    in_specs = (rows, rows, rows, P(), P(), P("dp", SAMPLE_AXES), P("dp", None), P())
    out_specs = (rows, rows, P(ALL_AXES, None), P(ALL_AXES, None))
    return jax.shard_map(body, mesh=fine, in_specs=in_specs, out_specs=out_specs, check_vma=False)
```
